512 devices in a mesh: cfg: 2 (over y_lo), seq: 128 (over z, x, core), head: 2 (over y_hi).
Axes of the slice: x: 4, y: 4 (y_hi: 2, y_lo: 2; y = y_hi * 2 + y_lo), z: 16, core: 2. Of those that a mesh axis runs over, the one named last changes fastest.
Arguments:
- queries: bfloat16 [2, 4096, 20, 128], P('cfg', 'seq', 'head'), may hold values from -16 to 16
- self_keys: bfloat16 [2, 4096, 20, 128], P('cfg', 'seq', 'head'), may hold values from -16 to 16
- self_values: bfloat16 [2, 4096, 20, 128], P('cfg', 'seq', 'head'), may hold values from -6 to 6
- cross_queries: bfloat16 [2, 4096, 20, 128], P('cfg', 'seq', 'head'), may hold values from -16 to 16
- text_keys: bfloat16 [2, 512, 20, 128], P('cfg', None, 'head'), may hold values from -16 to 16
- text_values: bfloat16 [2, 512, 20, 128], P('cfg', None, 'head'), may hold values from -6 to 6
- out_weight: bfloat16 [20, 128, 64], P('head'), may hold values from -0.5 to 0.5
- latent: float32 [4096, 64], P('seq', 'cfg'), may hold values from -6 to 6
Outputs:
- guided: float32 [4096, 64], P('seq', 'cfg')
- latent_next: float32 [4096, 64], P('seq', 'cfg')
The draws below stay inside these ranges and needn't reach their ends.
All inputs are finite; a program needn't handle non-finite values.
Results may differ from the reference program's by a relative error of at most 0.013.
Values may be sent and summed in bfloat16 or wider, within the bound.
No kernel may reach another device: no remote copies, remote signals or barrier semaphores. Data moves between devices by JAX's collectives and lax.ppermute only.
A program may use at most 128 MiB of HBM per device.

```python
import math
import jax
import jax.numpy as jnp
from jax import lax

HEADS = 20
HEAD_DIM = 128
TEXT_LEN = 512
PATCH_OUT = 64
LENGTH = 4096


def video_base(key):
    return jax.random.normal(key, (2, LENGTH, HEADS, HEAD_DIM), jnp.float32)


def text_base(key):
    return jax.random.normal(jax.random.fold_in(key, 101), (2, TEXT_LEN, HEADS, HEAD_DIM), jnp.float32)


def draw_queries(key, part):
    base = video_base(key)
    key = jax.random.fold_in(key, 3)
    fresh = jax.random.normal(key, base.shape, jnp.float32)
    fresh = jnp.clip(fresh, -6.0, 6.0)
    return jnp.clip(fresh, -16.0, 16.0).astype(jnp.bfloat16)


def draw_self_keys(key, part):
    base = video_base(key)
    key = jax.random.fold_in(key, 7)
    fresh = jax.random.normal(key, base.shape, jnp.float32)
    fresh = jnp.clip(fresh, -6.0, 6.0)
    return jnp.clip(fresh, -16.0, 16.0).astype(jnp.bfloat16)


def draw_cross_queries(key, part):
    key = jax.random.fold_in(key, 11)
    fresh = jax.random.normal(key, (2, LENGTH, HEADS, HEAD_DIM), jnp.float32)
    fresh = jnp.clip(fresh, -6.0, 6.0)
    return jnp.clip(fresh, -16.0, 16.0).astype(jnp.bfloat16)


def draw_text_keys(key, part):
    base = text_base(key)
    key = jax.random.fold_in(key, 13)
    fresh = jax.random.normal(key, base.shape, jnp.float32)
    fresh = jnp.clip(fresh, -6.0, 6.0)
    return jnp.clip(fresh, -16.0, 16.0).astype(jnp.bfloat16)


def block_levels(own_key, shape, pieces, least, top_value):
    def one(axis_at, blocks):
        draws = jax.random.uniform(jax.random.fold_in(jax.random.fold_in(own_key, 6), axis_at), (blocks,), jnp.float32, least / len(pieces), top_value / len(pieces))
        return jnp.repeat(jnp.exp(draws), shape[axis_at] // blocks).reshape((-1,) + (1,) * (len(shape) - axis_at - 1))

    loudness = one(*pieces[0])
    for cut in pieces[1:]:
        loudness = loudness * one(*cut)
    return loudness


def gaussian(key, dims, deviation, most, cuts=(), kind=jnp.bfloat16):
    drawn = deviation * jax.random.normal(key, dims, jnp.float32)
    if cuts:
        drawn = drawn * block_levels(key, dims, cuts, -0.22, 0.18)
    return jnp.clip(drawn, -most, most).astype(kind)


def setup_inputs(seed: int = 0) -> dict:
    keys = jax.random.split(jax.random.key(seed), 9)
    queries = draw_queries(jax.random.fold_in(keys[8], 71), 0)
    self_keys = draw_self_keys(jax.random.fold_in(keys[8], 71), 0)
    self_values = gaussian(keys[2], (2, LENGTH, HEADS, HEAD_DIM), 1.0, 6.0, ((0, 2), (1, 128), (2, 2)))
    cross_queries = draw_cross_queries(jax.random.fold_in(keys[8], 71), 0)
    text_keys = draw_text_keys(jax.random.fold_in(keys[8], 71), 0)
    text_values = gaussian(keys[5], (2, TEXT_LEN, HEADS, HEAD_DIM), 1.0, 6.0, ((0, 2), (2, 2)))
    out_weight = gaussian(keys[6], (HEADS, HEAD_DIM, PATCH_OUT), HEAD_DIM ** -0.5, 0.5, ((0, 2),))
    latent = gaussian(keys[7], (LENGTH, PATCH_OUT), 1.0, 6.0, ((0, 128), (1, 2)), jnp.float32)
    return dict(queries=queries, self_keys=self_keys, self_values=self_values, cross_queries=cross_queries, text_keys=text_keys, text_values=text_values, out_weight=out_weight, latent=latent)


guidance = 5.0
step_size = 0.1


def attend(queries, keys_in, values_in):
    scores = jnp.einsum("qhd,khd->hqk", queries.astype(jnp.float32), keys_in.astype(jnp.float32)) * (HEAD_DIM ** -0.5)
    row_top = jnp.max(scores, axis=-1, keepdims=True)
    powers = jnp.exp(scores - row_top)
    row_total = jnp.sum(powers, axis=-1)
    rounded = lax.optimization_barrier(powers.astype(jnp.bfloat16)).astype(jnp.float32)
    summed = jnp.einsum("hqk,khd->qhd", rounded, values_in.astype(jnp.float32))
    return (summed / jnp.transpose(row_total)[:, :, None]).astype(jnp.bfloat16)


def branch_velocity(own_queries, own_keys, own_values, own_cross, own_text_keys, own_text_values, out_weight):
    block_rows = math.gcd(LENGTH, 512)
    grouped = own_queries.reshape(LENGTH // block_rows, block_rows, HEADS, HEAD_DIM)
    self_out = lax.map(lambda block: attend(block, own_keys, own_values), grouped)
    self_out = self_out.reshape(LENGTH, HEADS, HEAD_DIM)
    cross_out = attend(own_cross, own_text_keys, own_text_values)
    feature = (self_out.astype(jnp.float32) + cross_out.astype(jnp.float32)).astype(jnp.bfloat16)
    return jnp.einsum("qhd,hdp->qp", feature.astype(jnp.float32), out_weight.astype(jnp.float32))


def reference(queries, self_keys, self_values, cross_queries, text_keys, text_values, out_weight, latent):
    cond = branch_velocity(queries[0], self_keys[0], self_values[0], cross_queries[0], text_keys[0], text_values[0], out_weight)
    uncond = branch_velocity(queries[1], self_keys[1], self_values[1], cross_queries[1], text_keys[1], text_values[1], out_weight)
    guided = uncond + guidance * (cond - uncond)
    return guided, latent + step_size * guided
```

```python
import math

import jax
import jax.numpy as jnp
from jax import lax
from jax.experimental import pallas as pl
from jax.experimental.pallas import tpu as pltpu
from jax.sharding import Mesh, PartitionSpec as P

HEAD_DIM = 128
HEADS_HERE = 10
ROWS = 32
SPREAD = 16
BLOCK = 80
KV_ROWS = 48
GUIDANCE = 5.0
STEP = 0.1
EXP2_SCALE = math.log2(math.e) / math.sqrt(HEAD_DIM)
VMEM_LIMIT = 56 * 1024 * 1024


def vmem():
    return pl.BlockSpec(memory_space=pltpu.VMEM)


def params():
    return pltpu.CompilerParams(vmem_limit_bytes=VMEM_LIMIT)


def pack_kernel(q_ref, k_ref, v_ref, w_ref, out_ref):
    for h in range(HEADS_HERE):
        out_ref[h, 0:32, :] = q_ref[h]
        out_ref[h, 32:64, :] = k_ref[h]
        projected = lax.dot_general(
            v_ref[h], w_ref[h], (((1,), (1,)), ((), ())), preferred_element_type=jnp.float32
        )
        packed = jnp.concatenate([projected[0:16], projected[16:32]], axis=1)
        out_ref[h, 64:80, :] = packed.astype(jnp.bfloat16)
    for h in range(HEADS_HERE, SPREAD):
        out_ref[h] = jnp.zeros((BLOCK, HEAD_DIM), jnp.bfloat16)


def pack(q, k, v, w):
    return pl.pallas_call(
        pack_kernel,
        out_shape=jax.ShapeDtypeStruct((SPREAD, BLOCK, HEAD_DIM), jnp.bfloat16),
        in_specs=[vmem()] * 4,
        out_specs=vmem(),
        compiler_params=params(),
        name="pack",
    )(q, k, v, w)


def scores(q, keys):
    return lax.dot_general(q, keys, (((1,), (1,)), ((), ())), preferred_element_type=jnp.float32)


def attend_kernel(where_ref, recv_ref, own_ref, other_ref, cross_ref, out_ref, total_ref):
    z = where_ref[0]
    branch = where_ref[1]
    active = z < HEADS_HERE
    keys, values = [], []
    for ref in (own_ref, other_ref):
        keys.append((ref[:, 0:16, :].reshape(1024, HEAD_DIM), ref[:, 16:32, :].reshape(1024, HEAD_DIM)))
        values.append(ref[:, 32:48, :].reshape(1024, HEAD_DIM))
    step = 256
    for first in range(0, SPREAD * ROWS, step):
        q = recv_ref[first // ROWS:(first + step) // ROWS, 0:32, :].reshape(step, HEAD_DIM)
        found = [[scores(q, part) for part in pair] for pair in keys]
        top = None
        for pair in found:
            for s in pair:
                t = jnp.max(s, axis=1, keepdims=True)
                top = t if top is None else jnp.maximum(top, t)
        top = top * EXP2_SCALE
        weight_sum = jnp.zeros((step, 1), jnp.float32)
        halves = [jnp.zeros((step, HEAD_DIM), jnp.float32) for _ in range(2)]
        for pair, value in zip(found, values):
            for i, s in enumerate(pair):
                p = jnp.exp2(s * EXP2_SCALE - top)
                weight_sum = weight_sum + jnp.sum(p, axis=1, keepdims=True)
                halves[i] = halves[i] + jnp.dot(p.astype(jnp.bfloat16), value, preferred_element_type=jnp.float32)
        summed = halves[0] + pltpu.roll(halves[1], 64, 1)
        total_ref[first:first + step, :] = jnp.where(active, summed / weight_sum, 0.0)
    mine = pl.ds(pl.multiple_of(z * ROWS, ROWS), ROWS)
    total_ref[mine, :] = total_ref[mine, :] + cross_ref[...]
    total = total_ref[...] * jnp.where(branch == 0, GUIDANCE, 1.0 - GUIDANCE)
    total = total.reshape(SPREAD, 4, 8, HEAD_DIM)
    lane_group = lax.broadcasted_iota(jnp.int32, (SPREAD * 8, HEAD_DIM), 1) // 32
    blocks = []
    for half in range(2):
        block = jnp.zeros((SPREAD * 8, HEAD_DIM), jnp.float32)
        for g in range(4):
            piece = total[:, g].reshape(SPREAD * 8, HEAD_DIM)
            shift = (32 * g - 32 * half) % HEAD_DIM
            if shift:
                piece = pltpu.roll(piece, shift, 1)
            block = jnp.where(lane_group == g, piece, block)
        blocks.append(block.reshape(SPREAD, 1, 8, HEAD_DIM))
    out = jnp.concatenate([blocks[0], blocks[0], blocks[1], blocks[1]], axis=1)
    out_ref[...] = out.reshape(SPREAD * 32, HEAD_DIM).astype(jnp.bfloat16)


def attend(where, recv, own, other, cross):
    return pl.pallas_call(
        attend_kernel,
        out_shape=jax.ShapeDtypeStruct((SPREAD * 32, HEAD_DIM), jnp.bfloat16),
        in_specs=[pl.BlockSpec(memory_space=pltpu.SMEM)] + [vmem()] * 4,
        out_specs=vmem(),
        scratch_shapes=[pltpu.VMEM((SPREAD * ROWS, HEAD_DIM), jnp.float32)],
        compiler_params=params(),
        name="attend",
    )(where, recv, own, other, cross)


def finish_kernel(parts_ref, latent_ref, guided_ref, next_ref):
    parts = parts_ref[...].astype(jnp.float32).reshape(64, 8, HEAD_DIM)
    summed = jnp.sum(parts, axis=0)
    pieces = [summed] + [pltpu.roll(summed, HEAD_DIM - 32 * g, 1) for g in range(1, 4)]
    for g, piece in enumerate(pieces):
        rows = slice(8 * g, 8 * g + 8)
        guided_ref[rows, :] = piece[:, 0:32]
        next_ref[rows, :] = latent_ref[rows, :] + STEP * piece[:, 0:32]


def finish(parts, latent):
    shape = jax.ShapeDtypeStruct(latent.shape, jnp.float32)
    return pl.pallas_call(
        finish_kernel,
        out_shape=(shape, shape),
        in_specs=[vmem()] * 2,
        out_specs=(vmem(), vmem()),
        compiler_params=params(),
        name="finish",
    )(parts, latent)


def cross_velocity(queries, keys, values, w):
    s = jnp.einsum("hqd,hkd->hqk", queries, keys, preferred_element_type=jnp.float32) * HEAD_DIM ** (-0.5)
    top = jnp.max(s, axis=-1, keepdims=True)
    p = jnp.exp(s - top)
    out = jnp.einsum("hqk,hkd->hqd", p.astype(jnp.bfloat16), values, preferred_element_type=jnp.float32)
    out = (out / jnp.sum(p, axis=-1, keepdims=True)).astype(jnp.bfloat16)
    return jnp.einsum("hqd,hpd->qp", out, w, preferred_element_type=jnp.float32)


def heads_first(block):
    return jnp.transpose(block, (1, 0, 2))


def shards(queries, self_keys, self_values, cross_queries, text_keys, text_values, out_weight, latent):
    w = jnp.transpose(out_weight, (0, 2, 1))
    packed = pack(heads_first(queries[0]), heads_first(self_keys[0]), heads_first(self_values[0]), w)
    recv = lax.all_to_all(packed, "z", 0, 0, tiled=True)
    cross = cross_velocity(
        heads_first(cross_queries[0]), heads_first(text_keys[0]), heads_first(text_values[0]), w
    )
    cross = jnp.pad(cross, ((0, 0), (0, 64)))
    kv = jnp.broadcast_to(recv[None, :, 32:80, :], (4, SPREAD, KV_ROWS, HEAD_DIM))
    own = lax.all_to_all(kv, "x", 0, 0, tiled=True).reshape(64, KV_ROWS, HEAD_DIM)
    other = lax.ppermute(own, "c", [(0, 1), (1, 0)])
    where = jnp.stack([lax.axis_index("z"), lax.axis_index("cfg")]).astype(jnp.int32)
    back = attend(where, recv, own, other, cross)
    parts = lax.all_to_all(back, ("z", "cfg", "head"), 0, 0, tiled=True)
    return finish(parts, latent)


def solution(mesh):
    split = Mesh(mesh.devices.reshape(2, SPREAD, 4, 2, 2), ("cfg", "z", "x", "c", "head"))
    seq = ("z", "x", "c")
    tokens = P("cfg", seq, "head", None)
    text = P("cfg", None, "head", None)
    placed = (tokens, tokens, tokens, tokens, text, text, P("head", None, None), P(seq, "cfg"))
    return jax.shard_map(
        shards,
        mesh=split,
        in_specs=placed,
        out_specs=(P(seq, "cfg"), P(seq, "cfg")),
        check_vma=False,
    )
```

```python
import math

import jax
import jax.numpy as jnp
import numpy as np
from jax import lax
from jax.experimental import pallas as pl
from jax.experimental.pallas import tpu as pltpu
from jax.sharding import Mesh, PartitionSpec as P

HEAD_DIM = 128
HEADS_HERE = 10
ROWS = 32
SPREAD = 16
BLOCK = 80
KV_ROWS = 48
FIRST_PLANE = 10
PLANES = [(FIRST_PLANE + i) % SPREAD for i in range(SPREAD)]
AXES = ("cfg", "z", "x", "c", "head")
GUIDANCE = 5.0
STEP = 0.1
EXP2_SCALE = math.log2(math.e) / math.sqrt(HEAD_DIM)
VMEM_LIMIT = 36 * 1024 * 1024


def vmem():
    return pl.BlockSpec(memory_space=pltpu.VMEM)


def params():
    return pltpu.CompilerParams(vmem_limit_bytes=VMEM_LIMIT)


def pack_kernel(q_ref, k_ref, v_ref, w_ref, out_ref, blocks, v_scratch, w_scratch, sems):
    loads = [
        pltpu.make_async_copy(v_ref, v_scratch, sems.at[0]),
        pltpu.make_async_copy(w_ref, w_scratch, sems.at[1]),
        pltpu.make_async_copy(q_ref, blocks.at[0:HEADS_HERE, 0:32, :], sems.at[2]),
        pltpu.make_async_copy(k_ref, blocks.at[0:HEADS_HERE, 32:64, :], sems.at[3]),
    ]
    for load in loads:
        load.start()
    for h in range(HEADS_HERE, SPREAD):
        blocks[h] = jnp.zeros((BLOCK, HEAD_DIM), jnp.bfloat16)
    loads[0].wait()
    loads[1].wait()
    for h in range(HEADS_HERE):
        projected = lax.dot_general(
            v_scratch[h], w_scratch[h], (((1,), (1,)), ((), ())), preferred_element_type=jnp.float32
        )
        packed = jnp.concatenate([projected[0:16], projected[16:32]], axis=1)
        blocks[h, 64:80, :] = packed.astype(jnp.bfloat16)
    loads[2].wait()
    loads[3].wait()
    store = pltpu.make_async_copy(blocks, out_ref, sems.at[4])
    store.start()
    store.wait()


def pack(q, k, v, w):
    anywhere = pl.BlockSpec(memory_space=pl.ANY)
    return pl.pallas_call(
        pack_kernel,
        out_shape=jax.ShapeDtypeStruct((SPREAD, BLOCK, HEAD_DIM), jnp.bfloat16),
        in_specs=[anywhere] * 4,
        out_specs=anywhere,
        scratch_shapes=[
            pltpu.VMEM((SPREAD, BLOCK, HEAD_DIM), jnp.bfloat16),
            pltpu.VMEM((HEADS_HERE, ROWS, HEAD_DIM), jnp.bfloat16),
            pltpu.VMEM((HEADS_HERE, 64, HEAD_DIM), jnp.bfloat16),
            pltpu.SemaphoreType.DMA((5,)),
        ],
        compiler_params=pltpu.CompilerParams(vmem_limit_bytes=60 * 1024 * 1024),
        name="pack",
    )(q, k, v, w)


def cross_kernel(q_ref, k_ref, v_ref, w_ref, sum_ref, zero_ref):
    total = jnp.zeros((ROWS, 64), jnp.float32)
    for h in range(HEADS_HERE):
        s = scores(q_ref[h], k_ref[h])
        top = jnp.max(s, axis=1, keepdims=True) * EXP2_SCALE
        p = jnp.exp2(s * EXP2_SCALE - top)
        o = jnp.dot(p.astype(jnp.bfloat16), v_ref[h], preferred_element_type=jnp.float32)
        o = o / jnp.sum(p, axis=1, keepdims=True)
        total = total + scores(o.astype(jnp.bfloat16), w_ref[h])
    sum_ref[...] = jnp.concatenate([total, jnp.zeros((ROWS, 64), jnp.float32)], axis=1)
    zero_ref[0] = 0


def cross(q, k, v, w):
    return pl.pallas_call(
        cross_kernel,
        out_shape=(
            jax.ShapeDtypeStruct((ROWS, HEAD_DIM), jnp.float32),
            jax.ShapeDtypeStruct((1,), jnp.int32),
        ),
        in_specs=[vmem()] * 4,
        out_specs=(vmem(), pl.BlockSpec(memory_space=pltpu.SMEM)),
        compiler_params=params(),
        cost_estimate=pl.CostEstimate(flops=90_000_000, bytes_accessed=3_200_000, transcendentals=170_000),
        name="cross",
    )(q, k, v, w)


def scores(q, keys):
    return lax.dot_general(q, keys, (((1,), (1,)), ((), ())), preferred_element_type=jnp.float32)


def load_keys(ref):
    even, odd = ref[:, 0:16, :], ref[:, 16:32, :]
    return [part.reshape(1024, HEAD_DIM) for part in (even, odd)], ref[:, 32:48, :].reshape(1024, HEAD_DIM)


def half_attention(q, keys, value, found_top=None):
    found = [scores(q, part) for part in keys]
    top = jnp.max(jnp.maximum(found[0], found[1]), axis=1, keepdims=True) * EXP2_SCALE
    if found_top is not None:
        top = jnp.maximum(top, found_top)
    weights = [jnp.exp2(s * EXP2_SCALE - top) for s in found]
    weight_sum = jnp.sum(weights[0] + weights[1], axis=1, keepdims=True)
    even, odd = [jnp.dot(p.astype(jnp.bfloat16), value, preferred_element_type=jnp.float32) for p in weights]
    return even + pltpu.roll(odd, 64, 1), weight_sum, top


STEP_ROWS = 256


def first_kernel(q_ref, own_ref, sum_ref, stat_ref):
    keys, value = load_keys(own_ref)
    for first in range(0, SPREAD * ROWS, STEP_ROWS):
        rows = slice(first, first + STEP_ROWS)
        q = q_ref[first // ROWS:(first + STEP_ROWS) // ROWS, 0:32, :].reshape(STEP_ROWS, HEAD_DIM)
        summed, weight_sum, top = half_attention(q, keys, value)
        sum_ref[rows, :] = summed
        stat_ref[rows, :] = jnp.concatenate(
            [jnp.broadcast_to(weight_sum, (STEP_ROWS, 64)), jnp.broadcast_to(top, (STEP_ROWS, 64))], axis=1
        )


def first_half(recv, own):
    shape = jax.ShapeDtypeStruct((SPREAD * ROWS, HEAD_DIM), jnp.float32)
    return pl.pallas_call(
        first_kernel,
        out_shape=(shape, shape),
        in_specs=[vmem()] * 2,
        out_specs=(vmem(), vmem()),
        compiler_params=params(),
        cost_estimate=pl.CostEstimate(flops=540_000_000, bytes_accessed=1_600_000, transcendentals=1_000_000),
        name="first_half",
    )(recv, own)


def attend_kernel(where_ref, recv_ref, other_ref, sum_ref, stat_ref, cross_ref, out_ref, total_ref):
    slot = where_ref[0]
    branch = where_ref[1]
    active = slot < HEADS_HERE
    keys, value = load_keys(other_ref)
    for first in range(0, SPREAD * ROWS, STEP_ROWS):
        rows = slice(first, first + STEP_ROWS)
        q = recv_ref[first // ROWS:(first + STEP_ROWS) // ROWS, 0:32, :].reshape(STEP_ROWS, HEAD_DIM)
        first_sum, first_top = stat_ref[rows, 0:1], stat_ref[rows, 64:65]
        summed, weight_sum, top = half_attention(q, keys, value, first_top)
        scale = jnp.exp2(first_top - top)
        summed = summed + sum_ref[rows, :] * scale
        weight_sum = weight_sum + first_sum * scale
        total_ref[rows, :] = jnp.where(active, summed / weight_sum, 0.0)
    mine = pl.ds(pl.multiple_of(slot * ROWS, ROWS), ROWS)
    total_ref[mine, :] = total_ref[mine, :] + cross_ref[...]
    total = total_ref[...] * jnp.where(branch == 0, GUIDANCE, 1.0 - GUIDANCE)
    total = total.reshape(SPREAD, 4, 8, HEAD_DIM)
    lane_group = lax.broadcasted_iota(jnp.int32, (SPREAD * 8, HEAD_DIM), 1) // 32
    blocks = []
    for half in range(2):
        block = jnp.zeros((SPREAD * 8, HEAD_DIM), jnp.float32)
        for g in range(4):
            piece = total[:, g].reshape(SPREAD * 8, HEAD_DIM)
            shift = (32 * g - 32 * half) % HEAD_DIM
            if shift:
                piece = pltpu.roll(piece, shift, 1)
            block = jnp.where(lane_group == g, piece, block)
        blocks.append(block.reshape(SPREAD, 1, 8, HEAD_DIM))
    out = jnp.concatenate([blocks[0], blocks[0], blocks[1], blocks[1]], axis=1)
    out_ref[...] = out.reshape(SPREAD * 32, HEAD_DIM).astype(jnp.bfloat16)


def attend(where, recv, other, summed, stat, cross):
    return pl.pallas_call(
        attend_kernel,
        out_shape=jax.ShapeDtypeStruct((SPREAD * 32, HEAD_DIM), jnp.bfloat16),
        in_specs=[pl.BlockSpec(memory_space=pltpu.SMEM)] + [vmem()] * 5,
        out_specs=vmem(),
        scratch_shapes=[pltpu.VMEM((SPREAD * ROWS, HEAD_DIM), jnp.float32)],
        compiler_params=params(),
        name="attend",
    )(where, recv, other, summed, stat, cross)


def finish_kernel(parts_ref, latent_ref, guided_ref, next_ref):
    parts = parts_ref[...].astype(jnp.float32).reshape(64, 8, HEAD_DIM)
    summed = jnp.sum(parts, axis=0)
    pieces = [summed] + [pltpu.roll(summed, HEAD_DIM - 32 * g, 1) for g in range(1, 4)]
    for g, piece in enumerate(pieces):
        rows = slice(8 * g, 8 * g + 8)
        guided_ref[rows, :] = piece[:, 0:32]
        next_ref[rows, :] = latent_ref[rows, :] + STEP * piece[:, 0:32]


def finish(parts, latent):
    shape = jax.ShapeDtypeStruct(latent.shape, jnp.float32)
    return pl.pallas_call(
        finish_kernel,
        out_shape=(shape, shape),
        in_specs=[vmem()] * 2,
        out_specs=(vmem(), vmem()),
        compiler_params=params(),
        name="finish",
    )(parts, latent)


def back_groups():
    index = np.arange(512).reshape(2, SPREAD, 4, 2, 2)
    return [
        [int(index[f, z, x, c, h]) for z in PLANES for f in range(2) for h in range(2)]
        for x in range(4)
        for c in range(2)
    ]


def heads_first(block):
    return jnp.transpose(block, (1, 0, 2))


def shards(queries, self_keys, self_values, cross_queries, text_keys, text_values, out_weight, latent):
    w = jnp.transpose(out_weight, (0, 2, 1))
    packed = pack(heads_first(queries[0]), heads_first(self_keys[0]), heads_first(self_values[0]), w)
    recv = lax.all_to_all(packed, "z", 0, 0, tiled=True, axis_index_groups=[PLANES])
    crossed, zero = cross(heads_first(cross_queries[0]), heads_first(text_keys[0]), heads_first(text_values[0]), w)
    kv = jnp.where(zero[0] == 0, recv[:, 32:80, :], jnp.zeros((), recv.dtype))
    kv = jnp.broadcast_to(kv[None], (4, SPREAD, KV_ROWS, HEAD_DIM))
    own = lax.all_to_all(kv, "x", 0, 0, tiled=True).reshape(64, KV_ROWS, HEAD_DIM)
    other = lax.ppermute(own, "c", [(0, 1), (1, 0)])
    summed, stat = first_half(recv, own)
    slot = lax.rem(lax.axis_index("z") + (SPREAD - FIRST_PLANE), SPREAD)
    where = jnp.stack([slot, lax.axis_index("cfg")]).astype(jnp.int32)
    back = attend(where, recv, other, summed, stat, crossed)
    parts = lax.all_to_all(back, AXES, 0, 0, tiled=True, axis_index_groups=back_groups())
    return finish(parts, latent)


def solution(mesh):
    split = Mesh(mesh.devices.reshape(2, SPREAD, 4, 2, 2), ("cfg", "z", "x", "c", "head"))
    seq = ("z", "x", "c")
    tokens = P("cfg", seq, "head", None)
    text = P("cfg", None, "head", None)
    placed = (tokens, tokens, tokens, tokens, text, text, P("head", None, None), P(seq, "cfg"))
    return jax.shard_map(
        shards,
        mesh=split,
        in_specs=placed,
        out_specs=(P(seq, "cfg"), P(seq, "cfg")),
        check_vma=False,
    )
```

```python
import math

import jax
import jax.numpy as jnp
import numpy as np
from jax import lax
from jax.experimental import pallas as pl
from jax.experimental.pallas import tpu as pltpu
from jax.sharding import Mesh, PartitionSpec as P

HEAD_DIM = 128
HEADS_HERE = 10
ROWS = 32
SPREAD = 16
BLOCK = 64
KV_ROWS = 48
FIRST_PLANE = 10
PLANES = [(FIRST_PLANE + i) % SPREAD for i in range(SPREAD)]
AXES = ("cfg", "z", "x", "c", "head")
GUIDANCE = 5.0
STEP = 0.1
EXP2_SCALE = math.log2(math.e) / math.sqrt(HEAD_DIM)
VMEM_LIMIT = 36 * 1024 * 1024


def vmem():
    return pl.BlockSpec(memory_space=pltpu.VMEM)


def params():
    return pltpu.CompilerParams(vmem_limit_bytes=VMEM_LIMIT)


def key_slot(head):
    return 3 * (head // 2) + 2 * (head % 2)


def pack_kernel(q_ref, k_ref, v_ref, w_ref, out_ref, blocks, q_scratch, k_scratch, v_scratch, w_scratch, sems):
    loads = [
        pltpu.make_async_copy(v_ref, v_scratch, sems.at[0]),
        pltpu.make_async_copy(w_ref, w_scratch, sems.at[1]),
        pltpu.make_async_copy(q_ref, q_scratch, sems.at[2]),
        pltpu.make_async_copy(k_ref, k_scratch, sems.at[3]),
    ]
    for load in loads:
        load.start()
    for h in range(HEADS_HERE):
        blocks[key_slot(h), KV_ROWS:BLOCK, :] = jnp.zeros((BLOCK - KV_ROWS, HEAD_DIM), jnp.bfloat16)
    blocks[SPREAD - 1] = jnp.zeros((BLOCK, HEAD_DIM), jnp.bfloat16)
    for load in loads:
        load.wait()
    for h in range(HEADS_HERE):
        blocks[key_slot(h), 0:32, :] = k_scratch[h]
        blocks[3 * (h // 2) + 1, 32 * (h % 2):32 * (h % 2) + 32, :] = q_scratch[h]
        projected = lax.dot_general(
            v_scratch[h], w_scratch[h], (((1,), (1,)), ((), ())), preferred_element_type=jnp.float32
        )
        packed = jnp.concatenate([projected[0:16], projected[16:32]], axis=1)
        blocks[key_slot(h), 32:KV_ROWS, :] = packed.astype(jnp.bfloat16)
    store = pltpu.make_async_copy(blocks, out_ref, sems.at[4])
    store.start()
    store.wait()


def pack(q, k, v, w):
    anywhere = pl.BlockSpec(memory_space=pl.ANY)
    return pl.pallas_call(
        pack_kernel,
        out_shape=jax.ShapeDtypeStruct((SPREAD, BLOCK, HEAD_DIM), jnp.bfloat16),
        in_specs=[anywhere] * 4,
        out_specs=anywhere,
        scratch_shapes=[
            pltpu.VMEM((SPREAD, BLOCK, HEAD_DIM), jnp.bfloat16),
            pltpu.VMEM((HEADS_HERE, ROWS, HEAD_DIM), jnp.bfloat16),
            pltpu.VMEM((HEADS_HERE, ROWS, HEAD_DIM), jnp.bfloat16),
            pltpu.VMEM((HEADS_HERE, ROWS, HEAD_DIM), jnp.bfloat16),
            pltpu.VMEM((HEADS_HERE, 64, HEAD_DIM), jnp.bfloat16),
            pltpu.SemaphoreType.DMA((5,)),
        ],
        compiler_params=pltpu.CompilerParams(vmem_limit_bytes=60 * 1024 * 1024),
        name="pack",
    )(q, k, v, w)


def cross_kernel(q_ref, k_ref, v_ref, w_ref, sum_ref, zero_ref):
    total = jnp.zeros((ROWS, 64), jnp.float32)
    for h in range(HEADS_HERE):
        s = scores(q_ref[h], k_ref[h])
        top = jnp.max(s, axis=1, keepdims=True) * EXP2_SCALE
        p = jnp.exp2(s * EXP2_SCALE - top)
        o = jnp.dot(p.astype(jnp.bfloat16), v_ref[h], preferred_element_type=jnp.float32)
        o = o / jnp.sum(p, axis=1, keepdims=True)
        total = total + scores(o.astype(jnp.bfloat16), w_ref[h])
    columns = jnp.concatenate([total, jnp.zeros((ROWS, 64), jnp.float32)], axis=1).T
    columns = jnp.concatenate([columns, jnp.zeros((HEAD_DIM, HEAD_DIM - ROWS), jnp.float32)], axis=1)
    lane_group = lax.broadcasted_iota(jnp.int32, (8, HEAD_DIM), 1) // 32
    for half in range(2):
        block = columns[32 * half:32 * half + 8]
        for g in range(1, 4):
            piece = pltpu.roll(columns[32 * half + 8 * g:32 * half + 8 * g + 8], 32 * g, 1)
            block = jnp.where(lane_group == g, piece, block)
        sum_ref[16 * half:16 * half + 8, :] = block
        sum_ref[16 * half + 8:16 * half + 16, :] = block
    zero_ref[0] = 0


def cross(q, k, v, w):
    return pl.pallas_call(
        cross_kernel,
        out_shape=(
            jax.ShapeDtypeStruct((ROWS, HEAD_DIM), jnp.float32),
            jax.ShapeDtypeStruct((1,), jnp.int32),
        ),
        in_specs=[vmem()] * 4,
        out_specs=(vmem(), pl.BlockSpec(memory_space=pltpu.SMEM)),
        compiler_params=params(),
        cost_estimate=pl.CostEstimate(flops=90_000_000, bytes_accessed=3_200_000, transcendentals=170_000),
        name="cross",
    )(q, k, v, w)


def scores(q, keys):
    return lax.dot_general(q, keys, (((1,), (1,)), ((), ())), preferred_element_type=jnp.float32)


def load_keys(ref):
    even, odd = ref[:, 0:16, :], ref[:, 16:32, :]
    return [part.reshape(1024, HEAD_DIM) for part in (even, odd)], ref[:, 32:48, :].reshape(1024, HEAD_DIM)


def half_attention(q, keys, value, found_top=None):
    found = [scores(part, q) for part in keys]
    top = jnp.max(jnp.maximum(found[0], found[1]), axis=0, keepdims=True) * EXP2_SCALE
    if found_top is not None:
        top = jnp.maximum(top, found_top)
    weights = [jnp.exp2(s * EXP2_SCALE - top) for s in found]
    weight_sum = jnp.sum(weights[0] + weights[1], axis=0, keepdims=True)
    even, odd = [
        lax.dot_general(
            value, p.astype(jnp.bfloat16), (((0,), (0,)), ((), ())), preferred_element_type=jnp.float32
        )
        for p in weights
    ]
    return even[0:64] + odd[64:128], weight_sum, top


QUERIES = SPREAD * ROWS


def first_kernel(q_ref, own_ref, sum_ref, stat_ref):
    keys, value = load_keys(own_ref)
    summed, weight_sum, top = half_attention(q_ref[...].reshape(QUERIES, HEAD_DIM), keys, value)
    sum_ref[...] = summed
    stat_ref[0:8, :] = jnp.broadcast_to(weight_sum, (8, QUERIES))
    stat_ref[8:16, :] = jnp.broadcast_to(top, (8, QUERIES))


def first_half(q, own):
    return pl.pallas_call(
        first_kernel,
        out_shape=(
            jax.ShapeDtypeStruct((64, QUERIES), jnp.float32),
            jax.ShapeDtypeStruct((16, QUERIES), jnp.float32),
        ),
        in_specs=[vmem()] * 2,
        out_specs=(vmem(), vmem()),
        compiler_params=params(),
        cost_estimate=pl.CostEstimate(flops=540_000_000, bytes_accessed=1_600_000, transcendentals=1_000_000),
        name="first_half",
    )(q, own)


def attend_kernel(where_ref, q_ref, other_ref, sum_ref, stat_ref, cross_ref, out_ref, blocks):
    slot = where_ref[0]
    branch = where_ref[1]
    active = (slot < SPREAD - 1) & (where_ref[2] != 1)
    keys, value = load_keys(other_ref)
    first_sum, first_top = stat_ref[0:1, :], stat_ref[8:9, :]
    summed, weight_sum, top = half_attention(q_ref[...].reshape(QUERIES, HEAD_DIM), keys, value, first_top)
    scale = jnp.exp2(first_top - top)
    factor = jnp.where(branch == 0, GUIDANCE, 1.0 - GUIDANCE)
    total = (summed + sum_ref[...] * scale) * (factor / (weight_sum + first_sum * scale))
    total = jnp.where(active, total, 0.0)
    lane_group = lax.broadcasted_iota(jnp.int32, (32, HEAD_DIM), 1) // 32
    halves = []
    for half in range(2):
        groups = []
        for g in range(4):
            rows = total[32 * half + 8 * g:32 * half + 8 * g + 8]
            groups.append(jnp.concatenate([rows[:, 128 * t:128 * t + 128] for t in range(4)], axis=0))
        places = []
        for i in range(4):
            block = groups[i]
            for g in range(4):
                if g != i:
                    block = jnp.where(lane_group == g, pltpu.roll(groups[g], 32 * ((g - i) % 4), 1), block)
            places.append(block.reshape(4, 1, 1, 8, HEAD_DIM))
        halves.append(jnp.concatenate(places, axis=1))
    blocks[...] = jnp.concatenate([halves[0], halves[0], halves[1], halves[1]], axis=2).reshape(QUERIES, HEAD_DIM)
    mine = pl.ds(pl.multiple_of(slot * 32, 32), 32)
    blocks[mine, :] = blocks[mine, :] + cross_ref[...] * factor
    out_ref[...] = blocks[...].astype(jnp.bfloat16)


def attend(where, q, other, summed, stat, cross):
    return pl.pallas_call(
        attend_kernel,
        out_shape=jax.ShapeDtypeStruct((QUERIES, HEAD_DIM), jnp.bfloat16),
        in_specs=[pl.BlockSpec(memory_space=pltpu.SMEM)] + [vmem()] * 5,
        out_specs=vmem(),
        scratch_shapes=[pltpu.VMEM((QUERIES, HEAD_DIM), jnp.float32)],
        compiler_params=params(),
        name="attend",
    )(where, q, other, summed, stat, cross)


def finish_kernel(parts_ref, latent_ref, guided_ref, next_ref):
    parts = parts_ref[...].astype(jnp.float32).reshape(64, 8, HEAD_DIM)
    summed = jnp.sum(parts, axis=0)
    columns = jnp.concatenate([summed] + [pltpu.roll(summed, HEAD_DIM - 32 * g, 1) for g in range(1, 4)], axis=0)
    guided = columns.T[0:32]
    guided_ref[...] = guided
    next_ref[...] = latent_ref[...] + STEP * guided


def finish(parts, latent):
    shape = jax.ShapeDtypeStruct(latent.shape, jnp.float32)
    return pl.pallas_call(
        finish_kernel,
        out_shape=(shape, shape),
        in_specs=[vmem()] * 2,
        out_specs=(vmem(), vmem()),
        compiler_params=params(),
        name="finish",
    )(parts, latent)


def back_groups():
    index = np.arange(512).reshape(2, SPREAD, 4, 2, 2)
    return [
        [int(index[f, z, x, c, h]) for z in PLANES for f in range(2) for h in range(2)]
        for x in range(4)
        for c in range(2)
    ]


def heads_first(block):
    return jnp.transpose(block, (1, 0, 2))


def shards(queries, self_keys, self_values, cross_queries, text_keys, text_values, out_weight, latent):
    w = jnp.transpose(out_weight, (0, 2, 1))
    packed = pack(heads_first(queries[0]), heads_first(self_keys[0]), heads_first(self_values[0]), w)
    recv = lax.all_to_all(packed, "z", 0, 0, tiled=True, axis_index_groups=[PLANES])
    crossed, zero = cross(heads_first(cross_queries[0]), heads_first(text_keys[0]), heads_first(text_values[0]), w)
    kv = jnp.where(zero[0] == 0, recv[:, 0:KV_ROWS, :], jnp.zeros((), recv.dtype))
    kv = jnp.broadcast_to(kv[None], (4, SPREAD, KV_ROWS, HEAD_DIM))
    own = lax.all_to_all(kv, "x", 0, 0, tiled=True).reshape(64, KV_ROWS, HEAD_DIM)
    left = lax.ppermute(recv[:, 0:32, :], "z", [(PLANES[3 * i + 1], PLANES[3 * i]) for i in range(5)])
    right = lax.ppermute(recv[:, 32:64, :], "z", [(PLANES[3 * i + 1], PLANES[3 * i + 2]) for i in range(5)])
    slot = lax.rem(lax.axis_index("z") + (SPREAD - FIRST_PLANE), SPREAD)
    q = jnp.where(lax.rem(slot, 3) == 0, left, right)
    ready = q[0:1, 0:1, :] == q[0:1, 0:1, :]
    other = lax.ppermute(jnp.where(ready, own, jnp.zeros((), own.dtype)), "c", [(0, 1), (1, 0)])
    where = jnp.stack([slot, lax.axis_index("cfg"), lax.rem(slot, 3)]).astype(jnp.int32)
    summed, stat = first_half(q, own)
    back = attend(where, q, other, summed, stat, crossed)
    parts = lax.all_to_all(back, AXES, 0, 0, tiled=True, axis_index_groups=back_groups())
    return finish(parts, latent)


def solution(mesh):
    split = Mesh(mesh.devices.reshape(2, SPREAD, 4, 2, 2), ("cfg", "z", "x", "c", "head"))
    seq = ("z", "x", "c")
    tokens = P("cfg", seq, "head", None)
    text = P("cfg", None, "head", None)
    placed = (tokens, tokens, tokens, tokens, text, text, P("head", None, None), P(seq, "cfg"))
    return jax.shard_map(
        shards,
        mesh=split,
        in_specs=placed,
        out_specs=(P(seq, "cfg"), P(seq, "cfg")),
        check_vma=False,
    )
```

```python
import math

import jax
import jax.numpy as jnp
import numpy as np
from jax import lax
from jax.experimental import pallas as pl
from jax.experimental.pallas import tpu as pltpu
from jax.sharding import Mesh, PartitionSpec as P

HEAD_DIM = 128
HEADS_HERE = 10
ROWS = 32
SPREAD = 16
BLOCK = 56
KV_ROWS = 48
FIRST_PLANE = 10
BACK_PLANE = 8
PLANES = [(FIRST_PLANE + i) % SPREAD for i in range(SPREAD)]
BACK_PLANES = [(BACK_PLANE + i) % SPREAD for i in range(SPREAD)]
TURN = 32 * ((BACK_PLANE - FIRST_PLANE) % SPREAD)
AXES = ("cfg", "z", "x", "c", "head")
GUIDANCE = 5.0
STEP = 0.1
EXP2_SCALE = math.log2(math.e) / math.sqrt(HEAD_DIM)
VMEM_LIMIT = 36 * 1024 * 1024


def vmem():
    return pl.BlockSpec(memory_space=pltpu.VMEM)


def params():
    return pltpu.CompilerParams(vmem_limit_bytes=VMEM_LIMIT)


def key_slot(head):
    return 3 * (head // 2) + 2 * (head % 2)


def pack_kernel(q_ref, k_ref, v_ref, w_ref, out_ref, blocks, q_scratch, k_scratch, v_scratch, w_scratch, sems):
    loads = [
        pltpu.make_async_copy(v_ref, v_scratch, sems.at[0]),
        pltpu.make_async_copy(w_ref, w_scratch, sems.at[1]),
        pltpu.make_async_copy(q_ref, q_scratch, sems.at[2]),
        pltpu.make_async_copy(k_ref, k_scratch, sems.at[3]),
    ]
    for load in loads:
        load.start()
    for pair in range(HEADS_HERE // 2):
        blocks[3 * pair + 1, 48:BLOCK, :] = jnp.zeros((BLOCK - 48, HEAD_DIM), jnp.bfloat16)
    blocks[SPREAD - 1] = jnp.zeros((BLOCK, HEAD_DIM), jnp.bfloat16)
    for load in loads:
        load.wait()
    for h in range(HEADS_HERE):
        blocks[key_slot(h), 0:32, :] = k_scratch[h]
        blocks[key_slot(h), KV_ROWS:BLOCK, :] = q_scratch[h, 0:8]
        blocks[3 * (h // 2) + 1, 24 * (h % 2):24 * (h % 2) + 24, :] = q_scratch[h, 8:32]
        projected = lax.dot_general(
            v_scratch[h], w_scratch[h], (((1,), (1,)), ((), ())), preferred_element_type=jnp.float32
        )
        packed = jnp.concatenate([projected[0:16], projected[16:32]], axis=1)
        blocks[key_slot(h), 32:KV_ROWS, :] = packed.astype(jnp.bfloat16)
    store = pltpu.make_async_copy(blocks, out_ref, sems.at[4])
    store.start()
    store.wait()


def pack(q, k, v, w):
    anywhere = pl.BlockSpec(memory_space=pl.ANY)
    return pl.pallas_call(
        pack_kernel,
        out_shape=jax.ShapeDtypeStruct((SPREAD, BLOCK, HEAD_DIM), jnp.bfloat16),
        in_specs=[anywhere] * 4,
        out_specs=anywhere,
        scratch_shapes=[
            pltpu.VMEM((SPREAD, BLOCK, HEAD_DIM), jnp.bfloat16),
            pltpu.VMEM((HEADS_HERE, ROWS, HEAD_DIM), jnp.bfloat16),
            pltpu.VMEM((HEADS_HERE, ROWS, HEAD_DIM), jnp.bfloat16),
            pltpu.VMEM((HEADS_HERE, ROWS, HEAD_DIM), jnp.bfloat16),
            pltpu.VMEM((HEADS_HERE, 64, HEAD_DIM), jnp.bfloat16),
            pltpu.SemaphoreType.DMA((5,)),
        ],
        compiler_params=pltpu.CompilerParams(vmem_limit_bytes=60 * 1024 * 1024),
        name="pack",
    )(q, k, v, w)


def cross_kernel(q_ref, k_ref, v_ref, w_ref, sum_ref, zero_ref):
    total = jnp.zeros((ROWS, 64), jnp.float32)
    for h in range(HEADS_HERE):
        s = scores(q_ref[h], k_ref[h])
        top = jnp.max(s, axis=1, keepdims=True) * EXP2_SCALE
        p = jnp.exp2(s * EXP2_SCALE - top)
        o = jnp.dot(p.astype(jnp.bfloat16), v_ref[h], preferred_element_type=jnp.float32)
        o = o / jnp.sum(p, axis=1, keepdims=True)
        total = total + scores(o.astype(jnp.bfloat16), w_ref[h])
    columns = jnp.concatenate([total, jnp.zeros((ROWS, 64), jnp.float32)], axis=1).T
    columns = jnp.concatenate([columns, jnp.zeros((HEAD_DIM, HEAD_DIM - ROWS), jnp.float32)], axis=1)
    lane_group = lax.broadcasted_iota(jnp.int32, (8, HEAD_DIM), 1) // 32
    for half in range(2):
        block = columns[32 * half:32 * half + 8]
        for g in range(1, 4):
            piece = pltpu.roll(columns[32 * half + 8 * g:32 * half + 8 * g + 8], 32 * g, 1)
            block = jnp.where(lane_group == g, piece, block)
        sum_ref[16 * half:16 * half + 8, :] = block
        sum_ref[16 * half + 8:16 * half + 16, :] = block
    zero_ref[0] = 0


def cross(q, k, v, w):
    return pl.pallas_call(
        cross_kernel,
        out_shape=(
            jax.ShapeDtypeStruct((ROWS, HEAD_DIM), jnp.float32),
            jax.ShapeDtypeStruct((1,), jnp.int32),
        ),
        in_specs=[vmem()] * 4,
        out_specs=(vmem(), pl.BlockSpec(memory_space=pltpu.SMEM)),
        compiler_params=params(),
        cost_estimate=pl.CostEstimate(flops=90_000_000, bytes_accessed=3_200_000, transcendentals=170_000),
        name="cross",
    )(q, k, v, w)


def scores(q, keys):
    return lax.dot_general(q, keys, (((1,), (1,)), ((), ())), preferred_element_type=jnp.float32)


def load_keys(ref):
    even, odd = ref[:, 0:16, :], ref[:, 16:32, :]
    return [part.reshape(1024, HEAD_DIM) for part in (even, odd)], ref[:, 32:48, :].reshape(1024, HEAD_DIM)


def half_attention(q, keys, value):
    found = [scores(part, q) for part in keys]
    top = jnp.max(jnp.maximum(found[0], found[1]), axis=0, keepdims=True) * EXP2_SCALE
    weights = [jnp.exp2(s * EXP2_SCALE - top) for s in found]
    weight_sum = jnp.sum(weights[0] + weights[1], axis=0, keepdims=True)
    even, odd = [
        lax.dot_general(
            value, p.astype(jnp.bfloat16), (((0,), (0,)), ((), ())), preferred_element_type=jnp.float32
        )
        for p in weights
    ]
    return even[0:64] + odd[64:128], weight_sum, top


QUERIES = SPREAD * ROWS


STATE = 80


def partial_kernel(where_ref, q_ref, own_ref, keep_ref, give_ref):
    keys, value = load_keys(own_ref)
    states = []
    for core in range(2):
        summed, weight_sum, top = half_attention(q_ref[core].reshape(QUERIES, HEAD_DIM), keys, value)
        stats = [jnp.broadcast_to(x, (8, QUERIES)) for x in (weight_sum, top)]
        states.append(jnp.concatenate([summed] + stats, axis=0))
    first = where_ref[4] == 0
    keep_ref[...] = jnp.where(first, states[0], states[1])
    give_ref[...] = jnp.where(first, states[1], states[0])


def partial_attention(where, q, own):
    shape = jax.ShapeDtypeStruct((STATE, QUERIES), jnp.float32)
    return pl.pallas_call(
        partial_kernel,
        out_shape=(shape, shape),
        in_specs=[pl.BlockSpec(memory_space=pltpu.SMEM)] + [vmem()] * 2,
        out_specs=(vmem(), vmem()),
        compiler_params=params(),
        cost_estimate=pl.CostEstimate(flops=1_080_000_000, bytes_accessed=1_600_000, transcendentals=2_000_000),
        name="partial_attention",
    )(where, q, own)


def join_kernel(where_ref, keep_ref, given_ref, cross_ref, out_ref, blocks):
    slot = where_ref[0]
    branch = where_ref[1]
    active = (slot < SPREAD - 1) & (where_ref[2] != 1)
    given = given_ref[1 - where_ref[4]]
    kept = keep_ref[...]
    top = jnp.maximum(kept[72:73], given[72:73])
    scales = [jnp.exp2(state[72:73] - top) for state in (kept, given)]
    weight_sum = kept[64:65] * scales[0] + given[64:65] * scales[1]
    factor = jnp.where(branch == 0, GUIDANCE, 1.0 - GUIDANCE)
    share = factor / weight_sum
    total = kept[0:64] * (scales[0] * share) + given[0:64] * (scales[1] * share)
    total = jnp.where(active, total, 0.0)
    lane_group = lax.broadcasted_iota(jnp.int32, (32, HEAD_DIM), 1) // 32
    halves = []
    for half in range(2):
        groups = []
        for g in range(4):
            rows = total[32 * half + 8 * g:32 * half + 8 * g + 8]
            groups.append(jnp.concatenate([rows[:, 128 * t:128 * t + 128] for t in range(4)], axis=0))
        places = []
        for i in range(4):
            block = groups[i]
            for g in range(4):
                if g != i:
                    block = jnp.where(lane_group == g, pltpu.roll(groups[g], 32 * ((g - i) % 4), 1), block)
            places.append(block.reshape(4, 1, 1, 8, HEAD_DIM))
        halves.append(jnp.concatenate(places, axis=1))
    packed = jnp.concatenate([halves[0], halves[0], halves[1], halves[1]], axis=2).reshape(QUERIES, HEAD_DIM)
    blocks[0:QUERIES - TURN, :] = packed[TURN:]
    if TURN:
        blocks[QUERIES - TURN:QUERIES, :] = packed[:TURN]
    mine = pl.ds(pl.multiple_of(where_ref[3] * 32, 32), 32)
    blocks[mine, :] = blocks[mine, :] + cross_ref[...] * factor
    out_ref[...] = blocks[...].astype(jnp.bfloat16)


def join(where, keep, given, cross):
    return pl.pallas_call(
        join_kernel,
        out_shape=jax.ShapeDtypeStruct((QUERIES, HEAD_DIM), jnp.bfloat16),
        in_specs=[pl.BlockSpec(memory_space=pltpu.SMEM)] + [vmem()] * 3,
        out_specs=vmem(),
        scratch_shapes=[pltpu.VMEM((QUERIES, HEAD_DIM), jnp.float32)],
        compiler_params=params(),
        name="join",
    )(where, keep, given, cross)


def finish_kernel(parts_ref, latent_ref, guided_ref, next_ref):
    parts = parts_ref[...].astype(jnp.float32).reshape(64, 8, HEAD_DIM)
    summed = jnp.sum(parts, axis=0)
    columns = jnp.concatenate([summed] + [pltpu.roll(summed, HEAD_DIM - 32 * g, 1) for g in range(1, 4)], axis=0)
    guided = columns.T[0:32]
    guided_ref[...] = guided
    next_ref[...] = latent_ref[...] + STEP * guided


def finish(parts, latent):
    shape = jax.ShapeDtypeStruct(latent.shape, jnp.float32)
    return pl.pallas_call(
        finish_kernel,
        out_shape=(shape, shape),
        in_specs=[vmem()] * 2,
        out_specs=(vmem(), vmem()),
        compiler_params=params(),
        name="finish",
    )(parts, latent)


def back_groups():
    index = np.arange(512).reshape(2, SPREAD, 4, 2, 2)
    return [
        [int(index[f, z, x, c, h]) for z in BACK_PLANES for f in range(2) for h in range(2)]
        for x in range(4)
        for c in range(2)
    ]


def heads_first(block):
    return jnp.transpose(block, (1, 0, 2))


def shards(queries, self_keys, self_values, cross_queries, text_keys, text_values, out_weight, latent):
    w = jnp.transpose(out_weight, (0, 2, 1))
    packed = pack(heads_first(queries[0]), heads_first(self_keys[0]), heads_first(self_values[0]), w)
    recv = lax.all_to_all(packed, "z", 0, 0, tiled=True, axis_index_groups=[PLANES])
    crossed, zero = cross(heads_first(cross_queries[0]), heads_first(text_keys[0]), heads_first(text_values[0]), w)
    kv = jnp.where(zero[0] == 0, recv[:, 0:KV_ROWS, :], jnp.zeros((), recv.dtype))
    kv = jnp.broadcast_to(kv[None], (4, SPREAD, KV_ROWS, HEAD_DIM))
    own = lax.all_to_all(kv, "x", 0, 0, tiled=True).reshape(64, KV_ROWS, HEAD_DIM)
    left = lax.ppermute(recv[:, 0:24, :], "z", [(PLANES[3 * i + 1], PLANES[3 * i]) for i in range(5)])
    right = lax.ppermute(recv[:, 24:48, :], "z", [(PLANES[3 * i + 1], PLANES[3 * i + 2]) for i in range(5)])
    slot = lax.rem(lax.axis_index("z") + (SPREAD - FIRST_PLANE), SPREAD)
    q = jnp.concatenate([recv[:, KV_ROWS:BLOCK, :], jnp.where(lax.rem(slot, 3) == 0, left, right)], axis=1)
    both = lax.all_gather(q, "c")
    back_slot = lax.rem(lax.axis_index("z") + (SPREAD - BACK_PLANE), SPREAD)
    where = jnp.stack([slot, lax.axis_index("cfg"), lax.rem(slot, 3), back_slot, lax.axis_index("c")]).astype(jnp.int32)
    keep, give = partial_attention(where, both, own)
    back = join(where, keep, lax.all_gather(give, "c"), crossed)
    parts = lax.all_to_all(back, AXES, 0, 0, tiled=True, axis_index_groups=back_groups())
    return finish(parts, latent)


def solution(mesh):
    split = Mesh(mesh.devices.reshape(2, SPREAD, 4, 2, 2), ("cfg", "z", "x", "c", "head"))
    seq = ("z", "x", "c")
    tokens = P("cfg", seq, "head", None)
    text = P("cfg", None, "head", None)
    placed = (tokens, tokens, tokens, tokens, text, text, P("head", None, None), P(seq, "cfg"))
    return jax.shard_map(
        shards,
        mesh=split,
        in_specs=placed,
        out_specs=(P(seq, "cfg"), P(seq, "cfg")),
        check_vma=False,
    )
```

```python
import math

import jax
import jax.numpy as jnp
import numpy as np
from jax import lax
from jax.experimental import pallas as pl
from jax.experimental.pallas import tpu as pltpu
from jax.sharding import Mesh, PartitionSpec as P

HEAD_DIM = 128
HEADS_HERE = 10
ROWS = 32
SPREAD = 16
BLOCK = 56
KV_ROWS = 48
FIRST_PLANE = 11
BACK_PLANE = 9
PLANES = [(FIRST_PLANE + i) % SPREAD for i in range(SPREAD)]
BACK_PLANES = [(BACK_PLANE + i) % SPREAD for i in range(SPREAD)]
TURN = 32 * ((BACK_PLANE - FIRST_PLANE) % SPREAD)
AXES = ("cfg", "z", "x", "c", "head")
GUIDANCE = 5.0
STEP = 0.1
EXP2_SCALE = math.log2(math.e) / math.sqrt(HEAD_DIM)
VMEM_LIMIT = 36 * 1024 * 1024


def vmem():
    return pl.BlockSpec(memory_space=pltpu.VMEM)


def params():
    return pltpu.CompilerParams(vmem_limit_bytes=VMEM_LIMIT)


def key_slot(head):
    return 3 * (head // 2) + 2 * (head % 2)


def pack_kernel(q_ref, k_ref, v_ref, w_ref, out_ref, blocks, q_scratch, k_scratch, v_scratch, w_scratch, sems):
    loads = [
        pltpu.make_async_copy(v_ref, v_scratch, sems.at[0]),
        pltpu.make_async_copy(w_ref, w_scratch, sems.at[1]),
        pltpu.make_async_copy(q_ref, q_scratch, sems.at[2]),
        pltpu.make_async_copy(k_ref, k_scratch, sems.at[3]),
    ]
    for load in loads:
        load.start()
    for pair in range(HEADS_HERE // 2):
        blocks[3 * pair + 1, 48:BLOCK, :] = jnp.zeros((BLOCK - 48, HEAD_DIM), jnp.bfloat16)
    blocks[SPREAD - 1] = jnp.zeros((BLOCK, HEAD_DIM), jnp.bfloat16)
    for load in loads:
        load.wait()
    for h in range(HEADS_HERE):
        blocks[key_slot(h), 0:32, :] = k_scratch[h]
        blocks[key_slot(h), KV_ROWS:BLOCK, :] = q_scratch[h, 0:8]
        blocks[3 * (h // 2) + 1, 24 * (h % 2):24 * (h % 2) + 24, :] = q_scratch[h, 8:32]
        projected = lax.dot_general(
            v_scratch[h], w_scratch[h], (((1,), (1,)), ((), ())), preferred_element_type=jnp.float32
        )
        packed = jnp.concatenate([projected[0:16], projected[16:32]], axis=1)
        blocks[key_slot(h), 32:KV_ROWS, :] = packed.astype(jnp.bfloat16)
    store = pltpu.make_async_copy(blocks, out_ref, sems.at[4])
    store.start()
    store.wait()


def pack(q, k, v, w):
    anywhere = pl.BlockSpec(memory_space=pl.ANY)
    return pl.pallas_call(
        pack_kernel,
        out_shape=jax.ShapeDtypeStruct((SPREAD, BLOCK, HEAD_DIM), jnp.bfloat16),
        in_specs=[anywhere] * 4,
        out_specs=anywhere,
        scratch_shapes=[
            pltpu.VMEM((SPREAD, BLOCK, HEAD_DIM), jnp.bfloat16),
            pltpu.VMEM((HEADS_HERE, ROWS, HEAD_DIM), jnp.bfloat16),
            pltpu.VMEM((HEADS_HERE, ROWS, HEAD_DIM), jnp.bfloat16),
            pltpu.VMEM((HEADS_HERE, ROWS, HEAD_DIM), jnp.bfloat16),
            pltpu.VMEM((HEADS_HERE, 64, HEAD_DIM), jnp.bfloat16),
            pltpu.SemaphoreType.DMA((5,)),
        ],
        compiler_params=pltpu.CompilerParams(vmem_limit_bytes=60 * 1024 * 1024),
        name="pack",
    )(q, k, v, w)


def cross_kernel(q_ref, k_ref, v_ref, w_ref, sum_ref, zero_ref):
    total = jnp.zeros((ROWS, 64), jnp.float32)
    for h in range(HEADS_HERE):
        s = scores(q_ref[h], k_ref[h])
        top = jnp.max(s, axis=1, keepdims=True) * EXP2_SCALE
        p = jnp.exp2(s * EXP2_SCALE - top)
        o = jnp.dot(p.astype(jnp.bfloat16), v_ref[h], preferred_element_type=jnp.float32)
        o = o / jnp.sum(p, axis=1, keepdims=True)
        total = total + scores(o.astype(jnp.bfloat16), w_ref[h])
    columns = jnp.concatenate([total, jnp.zeros((ROWS, 64), jnp.float32)], axis=1).T
    columns = jnp.concatenate([columns, jnp.zeros((HEAD_DIM, HEAD_DIM - ROWS), jnp.float32)], axis=1)
    lane_group = lax.broadcasted_iota(jnp.int32, (8, HEAD_DIM), 1) // 32
    for half in range(2):
        block = columns[32 * half:32 * half + 8]
        for g in range(1, 4):
            piece = pltpu.roll(columns[32 * half + 8 * g:32 * half + 8 * g + 8], 32 * g, 1)
            block = jnp.where(lane_group == g, piece, block)
        sum_ref[16 * half:16 * half + 8, :] = block
        sum_ref[16 * half + 8:16 * half + 16, :] = block
    zero_ref[0] = 0


def cross(q, k, v, w):
    return pl.pallas_call(
        cross_kernel,
        out_shape=(
            jax.ShapeDtypeStruct((ROWS, HEAD_DIM), jnp.float32),
            jax.ShapeDtypeStruct((1,), jnp.int32),
        ),
        in_specs=[vmem()] * 4,
        out_specs=(vmem(), pl.BlockSpec(memory_space=pltpu.SMEM)),
        compiler_params=params(),
        cost_estimate=pl.CostEstimate(flops=90_000_000, bytes_accessed=3_200_000, transcendentals=170_000),
        name="cross",
    )(q, k, v, w)


def scores(q, keys):
    return lax.dot_general(q, keys, (((1,), (1,)), ((), ())), preferred_element_type=jnp.float32)


def load_keys(ref):
    even, odd = ref[:, 0:16, :], ref[:, 16:32, :]
    return [part.reshape(1024, HEAD_DIM) for part in (even, odd)], ref[:, 32:48, :].reshape(1024, HEAD_DIM)


def half_attention(q, keys, value, found_top=None):
    found = [scores(part, q) for part in keys]
    top = jnp.max(jnp.maximum(found[0], found[1]), axis=0, keepdims=True) * EXP2_SCALE
    if found_top is not None:
        top = jnp.maximum(top, found_top)
    weights = [jnp.exp2(s * EXP2_SCALE - top) for s in found]
    weight_sum = jnp.sum(weights[0] + weights[1], axis=0, keepdims=True)
    even, odd = [
        lax.dot_general(
            value, p.astype(jnp.bfloat16), (((0,), (0,)), ((), ())), preferred_element_type=jnp.float32
        )
        for p in weights
    ]
    return even[0:64] + odd[64:128], weight_sum, top


QUERIES = SPREAD * ROWS


def first_kernel(q_ref, own_ref, sum_ref, stat_ref):
    keys, value = load_keys(own_ref)
    summed, weight_sum, top = half_attention(q_ref[...].reshape(QUERIES, HEAD_DIM), keys, value)
    sum_ref[...] = summed
    stat_ref[0:8, :] = jnp.broadcast_to(weight_sum, (8, QUERIES))
    stat_ref[8:16, :] = jnp.broadcast_to(top, (8, QUERIES))


def first_half(q, own):
    return pl.pallas_call(
        first_kernel,
        out_shape=(
            jax.ShapeDtypeStruct((64, QUERIES), jnp.float32),
            jax.ShapeDtypeStruct((16, QUERIES), jnp.float32),
        ),
        in_specs=[vmem()] * 2,
        out_specs=(vmem(), vmem()),
        compiler_params=params(),
        cost_estimate=pl.CostEstimate(flops=540_000_000, bytes_accessed=1_600_000, transcendentals=1_000_000),
        name="first_half",
    )(q, own)


def attend_kernel(where_ref, q_ref, other_ref, sum_ref, stat_ref, cross_ref, out_ref, blocks):
    slot = where_ref[0]
    branch = where_ref[1]
    active = (slot < SPREAD - 1) & (where_ref[2] != 1)
    keys, value = load_keys(other_ref)
    first_sum, first_top = stat_ref[0:1, :], stat_ref[8:9, :]
    summed, weight_sum, top = half_attention(q_ref[...].reshape(QUERIES, HEAD_DIM), keys, value, first_top)
    scale = jnp.exp2(first_top - top)
    factor = jnp.where(branch == 0, GUIDANCE, 1.0 - GUIDANCE)
    total = (summed + sum_ref[...] * scale) * (factor / (weight_sum + first_sum * scale))
    total = jnp.where(active, total, 0.0)
    lane_group = lax.broadcasted_iota(jnp.int32, (32, HEAD_DIM), 1) // 32
    halves = []
    for half in range(2):
        groups = []
        for g in range(4):
            rows = total[32 * half + 8 * g:32 * half + 8 * g + 8]
            groups.append(jnp.concatenate([rows[:, 128 * t:128 * t + 128] for t in range(4)], axis=0))
        places = []
        for i in range(4):
            block = groups[i]
            for g in range(4):
                if g != i:
                    block = jnp.where(lane_group == g, pltpu.roll(groups[g], 32 * ((g - i) % 4), 1), block)
            places.append(block.reshape(4, 1, 1, 8, HEAD_DIM))
        halves.append(jnp.concatenate(places, axis=1))
    packed = jnp.concatenate([halves[0], halves[0], halves[1], halves[1]], axis=2).reshape(QUERIES, HEAD_DIM)
    blocks[0:QUERIES - TURN, :] = packed[TURN:]
    if TURN:
        blocks[QUERIES - TURN:QUERIES, :] = packed[:TURN]
    mine = pl.ds(pl.multiple_of(where_ref[3] * 32, 32), 32)
    blocks[mine, :] = blocks[mine, :] + cross_ref[...] * factor
    out_ref[...] = blocks[...].astype(jnp.bfloat16)


def attend(where, q, other, summed, stat, cross):
    return pl.pallas_call(
        attend_kernel,
        out_shape=jax.ShapeDtypeStruct((QUERIES, HEAD_DIM), jnp.bfloat16),
        in_specs=[pl.BlockSpec(memory_space=pltpu.SMEM)] + [vmem()] * 5,
        out_specs=vmem(),
        scratch_shapes=[pltpu.VMEM((QUERIES, HEAD_DIM), jnp.float32)],
        compiler_params=params(),
        name="attend",
    )(where, q, other, summed, stat, cross)


def finish_kernel(parts_ref, latent_ref, guided_ref, next_ref):
    parts = parts_ref[...].astype(jnp.float32).reshape(64, 8, HEAD_DIM)
    summed = jnp.sum(parts, axis=0)
    columns = jnp.concatenate([summed] + [pltpu.roll(summed, HEAD_DIM - 32 * g, 1) for g in range(1, 4)], axis=0)
    guided = columns.T[0:32]
    guided_ref[...] = guided
    next_ref[...] = latent_ref[...] + STEP * guided


def finish(parts, latent):
    shape = jax.ShapeDtypeStruct(latent.shape, jnp.float32)
    return pl.pallas_call(
        finish_kernel,
        out_shape=(shape, shape),
        in_specs=[vmem()] * 2,
        out_specs=(vmem(), vmem()),
        compiler_params=params(),
        name="finish",
    )(parts, latent)


def back_groups():
    index = np.arange(512).reshape(2, SPREAD, 4, 2, 2)
    return [
        [int(index[f, z, x, c, h]) for z in BACK_PLANES for f in range(2) for h in range(2)]
        for x in range(4)
        for c in range(2)
    ]


def heads_first(block):
    return jnp.transpose(block, (1, 0, 2))


def shards(queries, self_keys, self_values, cross_queries, text_keys, text_values, out_weight, latent):
    w = jnp.transpose(out_weight, (0, 2, 1))
    packed = pack(heads_first(queries[0]), heads_first(self_keys[0]), heads_first(self_values[0]), w)
    recv = lax.all_to_all(packed, "z", 0, 0, tiled=True, axis_index_groups=[PLANES])
    crossed, zero = cross(heads_first(cross_queries[0]), heads_first(text_keys[0]), heads_first(text_values[0]), w)
    kv = jnp.where(zero[0] == 0, recv[:, 0:KV_ROWS, :], jnp.zeros((), recv.dtype))
    kv = jnp.broadcast_to(kv[None], (4, SPREAD, KV_ROWS, HEAD_DIM))
    own = lax.all_to_all(kv, "x", 0, 0, tiled=True).reshape(64, KV_ROWS, HEAD_DIM)
    left = lax.ppermute(recv[:, 0:24, :], "z", [(PLANES[3 * i + 1], PLANES[3 * i]) for i in range(5)])
    right = lax.ppermute(recv[:, 24:48, :], "z", [(PLANES[3 * i + 1], PLANES[3 * i + 2]) for i in range(5)])
    slot = lax.rem(lax.axis_index("z") + (SPREAD - FIRST_PLANE), SPREAD)
    moved = jnp.where(lax.rem(slot, 3) == 0, left, right)
    q = jnp.concatenate([recv[:, KV_ROWS:BLOCK, :], moved], axis=1)
    ready = moved[0:1, 0:1, :] == moved[0:1, 0:1, :]
    other = lax.ppermute(jnp.where(ready, own, jnp.zeros((), own.dtype)), "c", [(0, 1), (1, 0)])
    back_slot = lax.rem(lax.axis_index("z") + (SPREAD - BACK_PLANE), SPREAD)
    where = jnp.stack([slot, lax.axis_index("cfg"), lax.rem(slot, 3), back_slot]).astype(jnp.int32)
    summed, stat = first_half(q, own)
    back = attend(where, q, other, summed, stat, crossed)
    parts = lax.all_to_all(back, AXES, 0, 0, tiled=True, axis_index_groups=back_groups())
    return finish(parts, latent)


def solution(mesh):
    split = Mesh(mesh.devices.reshape(2, SPREAD, 4, 2, 2), ("cfg", "z", "x", "c", "head"))
    seq = ("z", "x", "c")
    tokens = P("cfg", seq, "head", None)
    text = P("cfg", None, "head", None)
    placed = (tokens, tokens, tokens, tokens, text, text, P("head", None, None), P(seq, "cfg"))
    return jax.shard_map(
        shards,
        mesh=split,
        in_specs=placed,
        out_specs=(P(seq, "cfg"), P(seq, "cfg")),
        check_vma=False,
    )
```

```python
import math

import jax
import jax.numpy as jnp
import numpy as np
from jax import lax
from jax.experimental import pallas as pl
from jax.experimental.pallas import tpu as pltpu
from jax.sharding import Mesh, PartitionSpec as P

HEAD_DIM = 128
HEADS_HERE = 10
ROWS = 32
SPREAD = 16
BLOCK = 56
KV_ROWS = 48
FIRST_PLANE = 11
BACK_PLANE = 9
PLANES = [(FIRST_PLANE + i) % SPREAD for i in range(SPREAD)]
BACK_PLANES = [(BACK_PLANE + i) % SPREAD for i in range(SPREAD)]
OUT_PLANES = [11, 12, 10, 13, 9, 14, 8, 15, 7, 0, 6, 1, 5, 2, 4, 3]
AXES = ("cfg", "z", "x", "c", "head")
GUIDANCE = 5.0
STEP = 0.1
EXP2_SCALE = math.log2(math.e) / math.sqrt(HEAD_DIM)
VMEM_LIMIT = 36 * 1024 * 1024


def vmem():
    return pl.BlockSpec(memory_space=pltpu.VMEM)


def params():
    return pltpu.CompilerParams(vmem_limit_bytes=VMEM_LIMIT)


def key_slot(head):
    return OUT_PLANES.index(PLANES[3 * (head // 2) + 2 * (head % 2)])


def query_slot(pair):
    return OUT_PLANES.index(PLANES[3 * pair + 1])


def pack_kernel(q_ref, k_ref, v_ref, w_ref, out_ref, blocks, q_scratch, k_scratch, v_scratch, w_scratch, sems):
    loads = [
        pltpu.make_async_copy(v_ref, v_scratch, sems.at[0]),
        pltpu.make_async_copy(w_ref, w_scratch, sems.at[1]),
        pltpu.make_async_copy(q_ref, q_scratch, sems.at[2]),
        pltpu.make_async_copy(k_ref, k_scratch, sems.at[3]),
    ]
    for load in loads:
        load.start()
    for pair in range(HEADS_HERE // 2):
        blocks[query_slot(pair), 48:BLOCK, :] = jnp.zeros((BLOCK - 48, HEAD_DIM), jnp.bfloat16)
    blocks[OUT_PLANES.index(PLANES[SPREAD - 1])] = jnp.zeros((BLOCK, HEAD_DIM), jnp.bfloat16)
    for load in loads:
        load.wait()
    for h in range(HEADS_HERE):
        blocks[key_slot(h), 0:32, :] = k_scratch[h]
        blocks[key_slot(h), KV_ROWS:BLOCK, :] = q_scratch[h, 0:8]
        blocks[query_slot(h // 2), 24 * (h % 2):24 * (h % 2) + 24, :] = q_scratch[h, 8:32]
        projected = lax.dot_general(
            v_scratch[h], w_scratch[h], (((1,), (1,)), ((), ())), preferred_element_type=jnp.float32
        )
        packed = jnp.concatenate([projected[0:16], projected[16:32]], axis=1)
        blocks[key_slot(h), 32:KV_ROWS, :] = packed.astype(jnp.bfloat16)
    store = pltpu.make_async_copy(blocks, out_ref, sems.at[4])
    store.start()
    store.wait()


def pack(q, k, v, w):
    anywhere = pl.BlockSpec(memory_space=pl.ANY)
    return pl.pallas_call(
        pack_kernel,
        out_shape=jax.ShapeDtypeStruct((SPREAD, BLOCK, HEAD_DIM), jnp.bfloat16),
        in_specs=[anywhere] * 4,
        out_specs=anywhere,
        scratch_shapes=[
            pltpu.VMEM((SPREAD, BLOCK, HEAD_DIM), jnp.bfloat16),
            pltpu.VMEM((HEADS_HERE, ROWS, HEAD_DIM), jnp.bfloat16),
            pltpu.VMEM((HEADS_HERE, ROWS, HEAD_DIM), jnp.bfloat16),
            pltpu.VMEM((HEADS_HERE, ROWS, HEAD_DIM), jnp.bfloat16),
            pltpu.VMEM((HEADS_HERE, 64, HEAD_DIM), jnp.bfloat16),
            pltpu.SemaphoreType.DMA((5,)),
        ],
        compiler_params=pltpu.CompilerParams(vmem_limit_bytes=60 * 1024 * 1024),
        name="pack",
    )(q, k, v, w)


def cross_kernel(q_ref, k_ref, v_ref, w_ref, sum_ref, zero_ref):
    total = jnp.zeros((ROWS, 64), jnp.float32)
    for h in range(HEADS_HERE):
        s = scores(q_ref[h], k_ref[h])
        top = jnp.max(s, axis=1, keepdims=True) * EXP2_SCALE
        p = jnp.exp2(s * EXP2_SCALE - top)
        o = jnp.dot(p.astype(jnp.bfloat16), v_ref[h], preferred_element_type=jnp.float32)
        o = o / jnp.sum(p, axis=1, keepdims=True)
        total = total + scores(o.astype(jnp.bfloat16), w_ref[h])
    columns = jnp.concatenate([total, jnp.zeros((ROWS, 64), jnp.float32)], axis=1).T
    columns = jnp.concatenate([columns, jnp.zeros((HEAD_DIM, HEAD_DIM - ROWS), jnp.float32)], axis=1)
    lane_group = lax.broadcasted_iota(jnp.int32, (8, HEAD_DIM), 1) // 32
    for half in range(2):
        block = columns[32 * half:32 * half + 8]
        for g in range(1, 4):
            piece = pltpu.roll(columns[32 * half + 8 * g:32 * half + 8 * g + 8], 32 * g, 1)
            block = jnp.where(lane_group == g, piece, block)
        sum_ref[16 * half:16 * half + 8, :] = block
        sum_ref[16 * half + 8:16 * half + 16, :] = block
    zero_ref[0] = 0


def cross(q, k, v, w):
    return pl.pallas_call(
        cross_kernel,
        out_shape=(
            jax.ShapeDtypeStruct((ROWS, HEAD_DIM), jnp.float32),
            jax.ShapeDtypeStruct((1,), jnp.int32),
        ),
        in_specs=[vmem()] * 4,
        out_specs=(vmem(), pl.BlockSpec(memory_space=pltpu.SMEM)),
        compiler_params=params(),
        cost_estimate=pl.CostEstimate(flops=90_000_000, bytes_accessed=3_200_000, transcendentals=170_000),
        name="cross",
    )(q, k, v, w)


def scores(q, keys):
    return lax.dot_general(q, keys, (((1,), (1,)), ((), ())), preferred_element_type=jnp.float32)


def load_keys(ref):
    even, odd = ref[:, 0:16, :], ref[:, 16:32, :]
    return [part.reshape(1024, HEAD_DIM) for part in (even, odd)], ref[:, 32:48, :].reshape(1024, HEAD_DIM)


def half_attention(q, keys, value, found_top=None):
    found = [scores(part, q) for part in keys]
    top = jnp.max(jnp.maximum(found[0], found[1]), axis=0, keepdims=True) * EXP2_SCALE
    if found_top is not None:
        top = jnp.maximum(top, found_top)
    weights = [jnp.exp2(s * EXP2_SCALE - top) for s in found]
    weight_sum = jnp.sum(weights[0] + weights[1], axis=0, keepdims=True)
    even, odd = [
        lax.dot_general(
            value, p.astype(jnp.bfloat16), (((0,), (0,)), ((), ())), preferred_element_type=jnp.float32
        )
        for p in weights
    ]
    return even[0:64] + odd[64:128], weight_sum, top


QUERIES = SPREAD * ROWS


def first_kernel(q_ref, own_ref, sum_ref, stat_ref):
    keys, value = load_keys(own_ref)
    summed, weight_sum, top = half_attention(q_ref[...].reshape(QUERIES, HEAD_DIM), keys, value)
    sum_ref[...] = summed
    stat_ref[0:8, :] = jnp.broadcast_to(weight_sum, (8, QUERIES))
    stat_ref[8:16, :] = jnp.broadcast_to(top, (8, QUERIES))


def first_half(q, own):
    return pl.pallas_call(
        first_kernel,
        out_shape=(
            jax.ShapeDtypeStruct((64, QUERIES), jnp.float32),
            jax.ShapeDtypeStruct((16, QUERIES), jnp.float32),
        ),
        in_specs=[vmem()] * 2,
        out_specs=(vmem(), vmem()),
        compiler_params=params(),
        cost_estimate=pl.CostEstimate(flops=540_000_000, bytes_accessed=1_600_000, transcendentals=1_000_000),
        name="first_half",
    )(q, own)


def attend_kernel(where_ref, q_ref, other_ref, sum_ref, stat_ref, cross_ref, out_ref, blocks):
    slot = where_ref[0]
    branch = where_ref[1]
    active = (slot < SPREAD - 1) & (where_ref[2] != 1)
    keys, value = load_keys(other_ref)
    first_sum, first_top = stat_ref[0:1, :], stat_ref[8:9, :]
    summed, weight_sum, top = half_attention(q_ref[...].reshape(QUERIES, HEAD_DIM), keys, value, first_top)
    scale = jnp.exp2(first_top - top)
    factor = jnp.where(branch == 0, GUIDANCE, 1.0 - GUIDANCE)
    total = (summed + sum_ref[...] * scale) * (factor / (weight_sum + first_sum * scale))
    total = jnp.where(active, total, 0.0)
    lane_group = lax.broadcasted_iota(jnp.int32, (32, HEAD_DIM), 1) // 32
    halves = []
    for half in range(2):
        groups = []
        for g in range(4):
            rows = total[32 * half + 8 * g:32 * half + 8 * g + 8]
            groups.append(jnp.concatenate([rows[:, 128 * t:128 * t + 128] for t in range(4)], axis=0))
        places = []
        for i in range(4):
            block = groups[i]
            for g in range(4):
                if g != i:
                    block = jnp.where(lane_group == g, pltpu.roll(groups[g], 32 * ((g - i) % 4), 1), block)
            places.append(block.reshape(4, 1, 1, 8, HEAD_DIM))
        halves.append(jnp.concatenate(places, axis=1))
    packed = jnp.concatenate([halves[0], halves[0], halves[1], halves[1]], axis=2).reshape(QUERIES, HEAD_DIM)
    for at, plane in enumerate(BACK_PLANES):
        held = 32 * OUT_PLANES.index(plane)
        blocks[32 * at:32 * at + 32, :] = packed[held:held + 32]
    mine = pl.ds(pl.multiple_of(where_ref[3] * 32, 32), 32)
    blocks[mine, :] = blocks[mine, :] + cross_ref[...] * factor
    out_ref[...] = blocks[...].astype(jnp.bfloat16)


def attend(where, q, other, summed, stat, cross):
    return pl.pallas_call(
        attend_kernel,
        out_shape=jax.ShapeDtypeStruct((QUERIES, HEAD_DIM), jnp.bfloat16),
        in_specs=[pl.BlockSpec(memory_space=pltpu.SMEM)] + [vmem()] * 5,
        out_specs=vmem(),
        scratch_shapes=[pltpu.VMEM((QUERIES, HEAD_DIM), jnp.float32)],
        compiler_params=params(),
        name="attend",
    )(where, q, other, summed, stat, cross)


def finish_kernel(parts_ref, latent_ref, guided_ref, next_ref):
    parts = parts_ref[...].astype(jnp.float32).reshape(64, 8, HEAD_DIM)
    summed = jnp.sum(parts, axis=0)
    columns = jnp.concatenate([summed] + [pltpu.roll(summed, HEAD_DIM - 32 * g, 1) for g in range(1, 4)], axis=0)
    guided = columns.T[0:32]
    guided_ref[...] = guided
    next_ref[...] = latent_ref[...] + STEP * guided


def finish(parts, latent):
    shape = jax.ShapeDtypeStruct(latent.shape, jnp.float32)
    return pl.pallas_call(
        finish_kernel,
        out_shape=(shape, shape),
        in_specs=[vmem()] * 2,
        out_specs=(vmem(), vmem()),
        compiler_params=params(),
        name="finish",
    )(parts, latent)


def back_groups():
    index = np.arange(512).reshape(2, SPREAD, 4, 2, 2)
    return [
        [int(index[f, z, x, c, h]) for z in BACK_PLANES for f in range(2) for h in range(2)]
        for x in range(4)
        for c in range(2)
    ]


def heads_first(block):
    return jnp.transpose(block, (1, 0, 2))


def shards(queries, self_keys, self_values, cross_queries, text_keys, text_values, out_weight, latent):
    w = jnp.transpose(out_weight, (0, 2, 1))
    packed = pack(heads_first(queries[0]), heads_first(self_keys[0]), heads_first(self_values[0]), w)
    recv = lax.all_to_all(packed, "z", 0, 0, tiled=True, axis_index_groups=[OUT_PLANES])
    crossed, zero = cross(heads_first(cross_queries[0]), heads_first(text_keys[0]), heads_first(text_values[0]), w)
    kv = jnp.where(zero[0] == 0, recv[:, 0:KV_ROWS, :], jnp.zeros((), recv.dtype))
    kv = jnp.broadcast_to(kv[None], (4, SPREAD, KV_ROWS, HEAD_DIM))
    own = lax.all_to_all(kv, "x", 0, 0, tiled=True).reshape(64, KV_ROWS, HEAD_DIM)
    left = lax.ppermute(recv[:, 0:24, :], "z", [(PLANES[3 * i + 1], PLANES[3 * i]) for i in range(5)])
    right = lax.ppermute(recv[:, 24:48, :], "z", [(PLANES[3 * i + 1], PLANES[3 * i + 2]) for i in range(5)])
    slot = lax.rem(lax.axis_index("z") + (SPREAD - FIRST_PLANE), SPREAD)
    moved = jnp.where(lax.rem(slot, 3) == 0, left, right)
    q = jnp.concatenate([recv[:, KV_ROWS:BLOCK, :], moved], axis=1)
    ready = moved[0:1, 0:1, :] == moved[0:1, 0:1, :]
    other = lax.ppermute(jnp.where(ready, own, jnp.zeros((), own.dtype)), "c", [(0, 1), (1, 0)])
    back_slot = lax.rem(lax.axis_index("z") + (SPREAD - BACK_PLANE), SPREAD)
    where = jnp.stack([slot, lax.axis_index("cfg"), lax.rem(slot, 3), back_slot]).astype(jnp.int32)
    summed, stat = first_half(q, own)
    back = attend(where, q, other, summed, stat, crossed)
    parts = lax.all_to_all(back, AXES, 0, 0, tiled=True, axis_index_groups=back_groups())
    return finish(parts, latent)


def solution(mesh):
    split = Mesh(mesh.devices.reshape(2, SPREAD, 4, 2, 2), ("cfg", "z", "x", "c", "head"))
    seq = ("z", "x", "c")
    tokens = P("cfg", seq, "head", None)
    text = P("cfg", None, "head", None)
    placed = (tokens, tokens, tokens, tokens, text, text, P("head", None, None), P(seq, "cfg"))
    return jax.shard_map(
        shards,
        mesh=split,
        in_specs=placed,
        out_specs=(P(seq, "cfg"), P(seq, "cfg")),
        check_vma=False,
    )
```

```python
import math

import jax
import jax.numpy as jnp
import numpy as np
from jax import lax
from jax.experimental import pallas as pl
from jax.experimental.pallas import tpu as pltpu
from jax.sharding import Mesh, PartitionSpec as P

HEAD_DIM = 128
HEADS_HERE = 10
ROWS = 32
SPREAD = 16
BLOCK = 56
KV_ROWS = 48
FIRST_PLANE = 11
BACK_PLANE = 9
PLANES = [(FIRST_PLANE + i) % SPREAD for i in range(SPREAD)]
BACK_PLANES = [(BACK_PLANE + i) % SPREAD for i in range(SPREAD)]
OUT_PLANES = [11, 12, 10, 13, 9, 14, 8, 15, 7, 0, 6, 1, 5, 2, 4, 3]
AXES = ("cfg", "z", "x", "c", "head")
GUIDANCE = 5.0
STEP = 0.1
EXP2_SCALE = math.log2(math.e) / math.sqrt(HEAD_DIM)
VMEM_LIMIT = 36 * 1024 * 1024


def vmem():
    return pl.BlockSpec(memory_space=pltpu.VMEM)


def params():
    return pltpu.CompilerParams(vmem_limit_bytes=VMEM_LIMIT)


def key_slot(head):
    return OUT_PLANES.index(PLANES[3 * (head // 2) + 2 * (head % 2)])


def query_slot(pair):
    return OUT_PLANES.index(PLANES[3 * pair + 1])


def pack_kernel(q_ref, k_ref, v_ref, w_ref, out_ref, blocks, q_scratch, k_scratch, v_scratch, w_scratch, sems):
    loads = [
        pltpu.make_async_copy(v_ref, v_scratch, sems.at[0]),
        pltpu.make_async_copy(w_ref, w_scratch, sems.at[1]),
        pltpu.make_async_copy(q_ref, q_scratch, sems.at[2]),
        pltpu.make_async_copy(k_ref, k_scratch, sems.at[3]),
    ]
    for load in loads:
        load.start()
    for pair in range(HEADS_HERE // 2):
        blocks[query_slot(pair), 48:BLOCK, :] = jnp.zeros((BLOCK - 48, HEAD_DIM), jnp.bfloat16)
    blocks[OUT_PLANES.index(PLANES[SPREAD - 1])] = jnp.zeros((BLOCK, HEAD_DIM), jnp.bfloat16)
    for load in loads:
        load.wait()
    for h in range(HEADS_HERE):
        blocks[key_slot(h), 0:32, :] = k_scratch[h]
        blocks[key_slot(h), KV_ROWS:BLOCK, :] = q_scratch[h, 0:8]
        blocks[query_slot(h // 2), 24 * (h % 2):24 * (h % 2) + 24, :] = q_scratch[h, 8:32]
        projected = lax.dot_general(
            v_scratch[h], w_scratch[h], (((1,), (1,)), ((), ())), preferred_element_type=jnp.float32
        )
        packed = jnp.concatenate([projected[0:16], projected[16:32]], axis=1)
        blocks[key_slot(h), 32:KV_ROWS, :] = packed.astype(jnp.bfloat16)
    store = pltpu.make_async_copy(blocks, out_ref, sems.at[4])
    store.start()
    store.wait()


def pack(q, k, v, w):
    anywhere = pl.BlockSpec(memory_space=pl.ANY)
    return pl.pallas_call(
        pack_kernel,
        out_shape=jax.ShapeDtypeStruct((SPREAD, BLOCK, HEAD_DIM), jnp.bfloat16),
        in_specs=[anywhere] * 4,
        out_specs=anywhere,
        scratch_shapes=[
            pltpu.VMEM((SPREAD, BLOCK, HEAD_DIM), jnp.bfloat16),
            pltpu.VMEM((HEADS_HERE, ROWS, HEAD_DIM), jnp.bfloat16),
            pltpu.VMEM((HEADS_HERE, ROWS, HEAD_DIM), jnp.bfloat16),
            pltpu.VMEM((HEADS_HERE, ROWS, HEAD_DIM), jnp.bfloat16),
            pltpu.VMEM((HEADS_HERE, 64, HEAD_DIM), jnp.bfloat16),
            pltpu.SemaphoreType.DMA((5,)),
        ],
        compiler_params=pltpu.CompilerParams(vmem_limit_bytes=60 * 1024 * 1024),
        name="pack",
    )(q, k, v, w)


def cross_kernel(q_ref, k_ref, v_ref, w_ref, sum_ref, zero_ref):
    total = jnp.zeros((ROWS, 64), jnp.float32)
    for h in range(HEADS_HERE):
        s = scores(q_ref[h], k_ref[h])
        top = jnp.max(s, axis=1, keepdims=True) * EXP2_SCALE
        p = jnp.exp2(s * EXP2_SCALE - top)
        o = jnp.dot(p.astype(jnp.bfloat16), v_ref[h], preferred_element_type=jnp.float32)
        o = o / jnp.sum(p, axis=1, keepdims=True)
        total = total + scores(o.astype(jnp.bfloat16), w_ref[h])
    columns = jnp.concatenate([total, jnp.zeros((ROWS, 64), jnp.float32)], axis=1).T
    columns = jnp.concatenate([columns, jnp.zeros((HEAD_DIM, HEAD_DIM - ROWS), jnp.float32)], axis=1)
    lane_group = lax.broadcasted_iota(jnp.int32, (8, HEAD_DIM), 1) // 32
    for half in range(2):
        block = columns[32 * half:32 * half + 8]
        for g in range(1, 4):
            piece = pltpu.roll(columns[32 * half + 8 * g:32 * half + 8 * g + 8], 32 * g, 1)
            block = jnp.where(lane_group == g, piece, block)
        sum_ref[16 * half:16 * half + 8, :] = block
        sum_ref[16 * half + 8:16 * half + 16, :] = block
    zero_ref[0] = 0


def cross(q, k, v, w):
    return pl.pallas_call(
        cross_kernel,
        out_shape=(
            jax.ShapeDtypeStruct((ROWS, HEAD_DIM), jnp.float32),
            jax.ShapeDtypeStruct((1,), jnp.int32),
        ),
        in_specs=[vmem()] * 4,
        out_specs=(vmem(), pl.BlockSpec(memory_space=pltpu.SMEM)),
        compiler_params=params(),
        cost_estimate=pl.CostEstimate(flops=90_000_000, bytes_accessed=3_200_000, transcendentals=170_000),
        name="cross",
    )(q, k, v, w)


def scores(q, keys):
    return lax.dot_general(q, keys, (((1,), (1,)), ((), ())), preferred_element_type=jnp.float32)


def load_keys(ref):
    even, odd = ref[:, 0:16, :], ref[:, 16:32, :]
    return [part.reshape(1024, HEAD_DIM) for part in (even, odd)], ref[:, 32:48, :].reshape(1024, HEAD_DIM)


def half_attention(q, keys, value, found_top=None):
    found = [scores(part, q) for part in keys]
    top = jnp.max(jnp.maximum(found[0], found[1]), axis=0, keepdims=True) * EXP2_SCALE
    if found_top is not None:
        top = jnp.maximum(top, found_top)
    weights = [jnp.exp2(s * EXP2_SCALE - top) for s in found]
    weight_sum = jnp.sum(weights[0] + weights[1], axis=0, keepdims=True)
    even, odd = [
        lax.dot_general(
            value, p.astype(jnp.bfloat16), (((0,), (0,)), ((), ())), preferred_element_type=jnp.float32
        )
        for p in weights
    ]
    return even[0:64] + odd[64:128], weight_sum, top


QUERIES = SPREAD * ROWS


def first_kernel(q_ref, own_ref, sum_ref, stat_ref):
    keys, value = load_keys(own_ref)
    summed, weight_sum, top = half_attention(q_ref[...].reshape(QUERIES, HEAD_DIM), keys, value)
    sum_ref[...] = summed
    stat_ref[0:8, :] = jnp.broadcast_to(weight_sum, (8, QUERIES))
    stat_ref[8:16, :] = jnp.broadcast_to(top, (8, QUERIES))


def first_half(q, own):
    return pl.pallas_call(
        first_kernel,
        out_shape=(
            jax.ShapeDtypeStruct((64, QUERIES), jnp.float32),
            jax.ShapeDtypeStruct((16, QUERIES), jnp.float32),
        ),
        in_specs=[vmem()] * 2,
        out_specs=(vmem(), vmem()),
        compiler_params=params(),
        cost_estimate=pl.CostEstimate(flops=540_000_000, bytes_accessed=1_600_000, transcendentals=1_000_000),
        name="first_half",
    )(q, own)


def attend_kernel(where_ref, q_ref, other_ref, sum_ref, stat_ref, cross_ref, out_ref, blocks):
    slot = where_ref[0]
    branch = where_ref[1]
    active = (slot < SPREAD - 1) & (where_ref[2] != 1)
    keys, value = load_keys(other_ref)
    first_sum, first_top = stat_ref[0:1, :], stat_ref[8:9, :]
    summed, weight_sum, top = half_attention(q_ref[...].reshape(QUERIES, HEAD_DIM), keys, value, first_top)
    scale = jnp.exp2(first_top - top)
    factor = jnp.where(branch == 0, GUIDANCE, 1.0 - GUIDANCE)
    total = (summed + sum_ref[...] * scale) * (factor / (weight_sum + first_sum * scale))
    total = jnp.where(active, total, 0.0)
    lane_group = lax.broadcasted_iota(jnp.int32, (32, HEAD_DIM), 1) // 32
    halves = []
    for half in range(2):
        groups = []
        for g in range(4):
            rows = total[32 * half + 8 * g:32 * half + 8 * g + 8]
            groups.append(jnp.concatenate([rows[:, 128 * t:128 * t + 128] for t in range(4)], axis=0))
        places = []
        for i in range(4):
            block = groups[i]
            for g in range(4):
                if g != i:
                    block = jnp.where(lane_group == g, pltpu.roll(groups[g], 32 * ((g - i) % 4), 1), block)
            places.append(block.reshape(4, 1, 1, 8, HEAD_DIM))
        halves.append(jnp.concatenate(places, axis=1))
    packed = jnp.concatenate([halves[0], halves[0], halves[1], halves[1]], axis=2).reshape(QUERIES, HEAD_DIM)
    for at, plane in enumerate(BACK_PLANES):
        held = 32 * OUT_PLANES.index(plane)
        blocks[32 * at:32 * at + 32, :] = packed[held:held + 32]
    mine = pl.ds(pl.multiple_of(where_ref[3] * 32, 32), 32)
    blocks[mine, :] = blocks[mine, :] + cross_ref[...] * factor
    out_ref[...] = blocks[...].astype(jnp.bfloat16)


def attend(where, q, other, summed, stat, cross):
    return pl.pallas_call(
        attend_kernel,
        out_shape=jax.ShapeDtypeStruct((QUERIES, HEAD_DIM), jnp.bfloat16),
        in_specs=[pl.BlockSpec(memory_space=pltpu.SMEM)] + [vmem()] * 5,
        out_specs=vmem(),
        scratch_shapes=[pltpu.VMEM((QUERIES, HEAD_DIM), jnp.float32)],
        compiler_params=params(),
        name="attend",
    )(where, q, other, summed, stat, cross)


def finish_kernel(parts_ref, latent_ref, guided_ref, next_ref):
    parts = parts_ref[...].astype(jnp.float32).reshape(64, 8, HEAD_DIM)
    summed = jnp.sum(parts, axis=0)
    columns = jnp.concatenate([summed] + [pltpu.roll(summed, HEAD_DIM - 32 * g, 1) for g in range(1, 4)], axis=0)
    guided = columns.T[0:32]
    guided_ref[...] = guided
    next_ref[...] = latent_ref[...] + STEP * guided


def finish(parts, latent):
    shape = jax.ShapeDtypeStruct(latent.shape, jnp.float32)
    return pl.pallas_call(
        finish_kernel,
        out_shape=(shape, shape),
        in_specs=[vmem()] * 2,
        out_specs=(vmem(), vmem()),
        compiler_params=params(),
        name="finish",
    )(parts, latent)


def back_groups():
    index = np.arange(512).reshape(2, SPREAD, 4, 2, 2)
    return [
        [int(index[f, z, x, c, h]) for z in BACK_PLANES for f in range(2) for h in range(2)]
        for x in range(4)
        for c in range(2)
    ]


def heads_first(block):
    return jnp.transpose(block, (1, 0, 2))


def shards(queries, self_keys, self_values, cross_queries, text_keys, text_values, out_weight, latent):
    w = jnp.transpose(out_weight, (0, 2, 1))
    packed = pack(heads_first(queries[0]), heads_first(self_keys[0]), heads_first(self_values[0]), w)
    recv = lax.all_to_all(packed, "z", 0, 0, tiled=True, axis_index_groups=[OUT_PLANES])
    crossed, zero = cross(heads_first(cross_queries[0]), heads_first(text_keys[0]), heads_first(text_values[0]), w)
    kv = jnp.broadcast_to(recv[None, :, 0:KV_ROWS, :], (4, SPREAD, KV_ROWS, HEAD_DIM))
    kv = jnp.where(zero[0] == 0, kv, jnp.zeros((), recv.dtype))
    own = lax.all_to_all(kv, "x", 0, 0, tiled=True).reshape(64, KV_ROWS, HEAD_DIM)
    left = lax.ppermute(recv[:, 0:24, :], "z", [(PLANES[3 * i + 1], PLANES[3 * i]) for i in range(5)])
    right = lax.ppermute(recv[:, 24:48, :], "z", [(PLANES[3 * i + 1], PLANES[3 * i + 2]) for i in range(5)])
    slot = lax.rem(lax.axis_index("z") + (SPREAD - FIRST_PLANE), SPREAD)
    moved = jnp.where(lax.rem(slot, 3) == 0, left, right)
    q = jnp.concatenate([recv[:, KV_ROWS:BLOCK, :], moved], axis=1)
    ready = moved[0:1, 0:1, :] == moved[0:1, 0:1, :]
    tile = jnp.where(ready, own[0:1, 0:16, :], jnp.zeros((), own.dtype))
    own = lax.dynamic_update_slice(own, tile, (0, 0, 0))
    other = lax.ppermute(own, "c", [(0, 1), (1, 0)])
    back_slot = lax.rem(lax.axis_index("z") + (SPREAD - BACK_PLANE), SPREAD)
    where = jnp.stack([slot, lax.axis_index("cfg"), lax.rem(slot, 3), back_slot]).astype(jnp.int32)
    summed, stat = first_half(q, own)
    back = attend(where, q, other, summed, stat, crossed)
    parts = lax.all_to_all(back, AXES, 0, 0, tiled=True, axis_index_groups=back_groups())
    return finish(parts, latent)


def solution(mesh):
    split = Mesh(mesh.devices.reshape(2, SPREAD, 4, 2, 2), ("cfg", "z", "x", "c", "head"))
    seq = ("z", "x", "c")
    tokens = P("cfg", seq, "head", None)
    text = P("cfg", None, "head", None)
    placed = (tokens, tokens, tokens, tokens, text, text, P("head", None, None), P(seq, "cfg"))
    return jax.shard_map(
        shards,
        mesh=split,
        in_specs=placed,
        out_specs=(P(seq, "cfg"), P(seq, "cfg")),
        check_vma=False,
    )
```

```python
import math

import jax
import jax.numpy as jnp
import numpy as np
from jax import lax
from jax.experimental import pallas as pl
from jax.experimental.pallas import tpu as pltpu
from jax.sharding import Mesh, PartitionSpec as P

HEAD_DIM = 128
HEADS_HERE = 10
ROWS = 32
SPREAD = 16
BLOCK = 56
KV_ROWS = 48
FIRST_PLANE = 11
BACK_PLANE = 9
PLANES = [(FIRST_PLANE + i) % SPREAD for i in range(SPREAD)]
BACK_PLANES = [(BACK_PLANE + i) % SPREAD for i in range(SPREAD)]
OUT_PLANES = [11, 12, 10, 13, 9, 8, 7, 6, 5, 4, 3, 2, 1, 0, 15, 14]
AXES = ("cfg", "z", "x", "c", "head")
GUIDANCE = 5.0
STEP = 0.1
EXP2_SCALE = math.log2(math.e) / math.sqrt(HEAD_DIM)
VMEM_LIMIT = 36 * 1024 * 1024


def vmem():
    return pl.BlockSpec(memory_space=pltpu.VMEM)


def params():
    return pltpu.CompilerParams(vmem_limit_bytes=VMEM_LIMIT)


def key_slot(head):
    return OUT_PLANES.index(PLANES[3 * (head // 2) + 2 * (head % 2)])


def query_slot(pair):
    return OUT_PLANES.index(PLANES[3 * pair + 1])


def pack_kernel(q_ref, k_ref, v_ref, w_ref, out_ref, blocks, q_scratch, k_scratch, v_scratch, w_scratch, sems):
    loads = [
        pltpu.make_async_copy(v_ref, v_scratch, sems.at[0]),
        pltpu.make_async_copy(w_ref, w_scratch, sems.at[1]),
        pltpu.make_async_copy(q_ref, q_scratch, sems.at[2]),
        pltpu.make_async_copy(k_ref, k_scratch, sems.at[3]),
    ]
    for load in loads:
        load.start()
    for pair in range(HEADS_HERE // 2):
        blocks[query_slot(pair), 48:BLOCK, :] = jnp.zeros((BLOCK - 48, HEAD_DIM), jnp.bfloat16)
    blocks[OUT_PLANES.index(PLANES[SPREAD - 1])] = jnp.zeros((BLOCK, HEAD_DIM), jnp.bfloat16)
    for load in loads:
        load.wait()
    for h in range(HEADS_HERE):
        blocks[key_slot(h), 0:32, :] = k_scratch[h]
        blocks[key_slot(h), KV_ROWS:BLOCK, :] = q_scratch[h, 0:8]
        blocks[query_slot(h // 2), 24 * (h % 2):24 * (h % 2) + 24, :] = q_scratch[h, 8:32]
        projected = lax.dot_general(
            v_scratch[h], w_scratch[h], (((1,), (1,)), ((), ())), preferred_element_type=jnp.float32
        )
        packed = jnp.concatenate([projected[0:16], projected[16:32]], axis=1)
        blocks[key_slot(h), 32:KV_ROWS, :] = packed.astype(jnp.bfloat16)
    store = pltpu.make_async_copy(blocks, out_ref, sems.at[4])
    store.start()
    store.wait()


def pack(q, k, v, w):
    anywhere = pl.BlockSpec(memory_space=pl.ANY)
    return pl.pallas_call(
        pack_kernel,
        out_shape=jax.ShapeDtypeStruct((SPREAD, BLOCK, HEAD_DIM), jnp.bfloat16),
        in_specs=[anywhere] * 4,
        out_specs=anywhere,
        scratch_shapes=[
            pltpu.VMEM((SPREAD, BLOCK, HEAD_DIM), jnp.bfloat16),
            pltpu.VMEM((HEADS_HERE, ROWS, HEAD_DIM), jnp.bfloat16),
            pltpu.VMEM((HEADS_HERE, ROWS, HEAD_DIM), jnp.bfloat16),
            pltpu.VMEM((HEADS_HERE, ROWS, HEAD_DIM), jnp.bfloat16),
            pltpu.VMEM((HEADS_HERE, 64, HEAD_DIM), jnp.bfloat16),
            pltpu.SemaphoreType.DMA((5,)),
        ],
        compiler_params=pltpu.CompilerParams(vmem_limit_bytes=60 * 1024 * 1024),
        name="pack",
    )(q, k, v, w)


def cross_kernel(q_ref, k_ref, v_ref, w_ref, sum_ref, zero_ref):
    total = jnp.zeros((ROWS, 64), jnp.float32)
    for h in range(HEADS_HERE):
        s = scores(q_ref[h], k_ref[h])
        top = jnp.max(s, axis=1, keepdims=True) * EXP2_SCALE
        p = jnp.exp2(s * EXP2_SCALE - top)
        o = jnp.dot(p.astype(jnp.bfloat16), v_ref[h], preferred_element_type=jnp.float32)
        o = o / jnp.sum(p, axis=1, keepdims=True)
        total = total + scores(o.astype(jnp.bfloat16), w_ref[h])
    columns = jnp.concatenate([total, jnp.zeros((ROWS, 64), jnp.float32)], axis=1).T
    columns = jnp.concatenate([columns, jnp.zeros((HEAD_DIM, HEAD_DIM - ROWS), jnp.float32)], axis=1)
    lane_group = lax.broadcasted_iota(jnp.int32, (8, HEAD_DIM), 1) // 32
    for half in range(2):
        block = columns[32 * half:32 * half + 8]
        for g in range(1, 4):
            piece = pltpu.roll(columns[32 * half + 8 * g:32 * half + 8 * g + 8], 32 * g, 1)
            block = jnp.where(lane_group == g, piece, block)
        sum_ref[16 * half:16 * half + 8, :] = block
        sum_ref[16 * half + 8:16 * half + 16, :] = block
    zero_ref[0] = 0


def cross(q, k, v, w):
    return pl.pallas_call(
        cross_kernel,
        out_shape=(
            jax.ShapeDtypeStruct((ROWS, HEAD_DIM), jnp.float32),
            jax.ShapeDtypeStruct((1,), jnp.int32),
        ),
        in_specs=[vmem()] * 4,
        out_specs=(vmem(), pl.BlockSpec(memory_space=pltpu.SMEM)),
        compiler_params=params(),
        cost_estimate=pl.CostEstimate(flops=90_000_000, bytes_accessed=3_200_000, transcendentals=170_000),
        name="cross",
    )(q, k, v, w)


def scores(q, keys):
    return lax.dot_general(q, keys, (((1,), (1,)), ((), ())), preferred_element_type=jnp.float32)


def load_keys(ref):
    even, odd = ref[:, 0:16, :], ref[:, 16:32, :]
    return [part.reshape(1024, HEAD_DIM) for part in (even, odd)], ref[:, 32:48, :].reshape(1024, HEAD_DIM)


def half_attention(q, keys, value, found_top=None):
    found = [scores(part, q) for part in keys]
    top = jnp.max(jnp.maximum(found[0], found[1]), axis=0, keepdims=True) * EXP2_SCALE
    if found_top is not None:
        top = jnp.maximum(top, found_top)
    weights = [jnp.exp2(s * EXP2_SCALE - top) for s in found]
    weight_sum = jnp.sum(weights[0] + weights[1], axis=0, keepdims=True)
    even, odd = [
        lax.dot_general(
            value, p.astype(jnp.bfloat16), (((0,), (0,)), ((), ())), preferred_element_type=jnp.float32
        )
        for p in weights
    ]
    return even[0:64] + odd[64:128], weight_sum, top


QUERIES = SPREAD * ROWS


def first_kernel(q_ref, own_ref, sum_ref, stat_ref):
    keys, value = load_keys(own_ref)
    summed, weight_sum, top = half_attention(q_ref[...].reshape(QUERIES, HEAD_DIM), keys, value)
    sum_ref[...] = summed
    stat_ref[0:8, :] = jnp.broadcast_to(weight_sum, (8, QUERIES))
    stat_ref[8:16, :] = jnp.broadcast_to(top, (8, QUERIES))


def first_half(q, own):
    return pl.pallas_call(
        first_kernel,
        out_shape=(
            jax.ShapeDtypeStruct((64, QUERIES), jnp.float32),
            jax.ShapeDtypeStruct((16, QUERIES), jnp.float32),
        ),
        in_specs=[vmem()] * 2,
        out_specs=(vmem(), vmem()),
        compiler_params=params(),
        cost_estimate=pl.CostEstimate(flops=540_000_000, bytes_accessed=1_600_000, transcendentals=1_000_000),
        name="first_half",
    )(q, own)


def attend_kernel(where_ref, q_ref, other_ref, sum_ref, stat_ref, cross_ref, out_ref, blocks):
    slot = where_ref[0]
    branch = where_ref[1]
    active = (slot < SPREAD - 1) & (where_ref[2] != 1)
    keys, value = load_keys(other_ref)
    first_sum, first_top = stat_ref[0:1, :], stat_ref[8:9, :]
    summed, weight_sum, top = half_attention(q_ref[...].reshape(QUERIES, HEAD_DIM), keys, value, first_top)
    scale = jnp.exp2(first_top - top)
    factor = jnp.where(branch == 0, GUIDANCE, 1.0 - GUIDANCE)
    total = (summed + sum_ref[...] * scale) * (factor / (weight_sum + first_sum * scale))
    total = jnp.where(active, total, 0.0)
    lane_group = lax.broadcasted_iota(jnp.int32, (32, HEAD_DIM), 1) // 32
    halves = []
    for half in range(2):
        groups = []
        for g in range(4):
            rows = total[32 * half + 8 * g:32 * half + 8 * g + 8]
            groups.append(jnp.concatenate([rows[:, 128 * t:128 * t + 128] for t in range(4)], axis=0))
        places = []
        for i in range(4):
            block = groups[i]
            for g in range(4):
                if g != i:
                    block = jnp.where(lane_group == g, pltpu.roll(groups[g], 32 * ((g - i) % 4), 1), block)
            places.append(block.reshape(4, 1, 1, 8, HEAD_DIM))
        halves.append(jnp.concatenate(places, axis=1))
    packed = jnp.concatenate([halves[0], halves[0], halves[1], halves[1]], axis=2).reshape(QUERIES, HEAD_DIM)
    for at, plane in enumerate(BACK_PLANES):
        held = 32 * OUT_PLANES.index(plane)
        blocks[32 * at:32 * at + 32, :] = packed[held:held + 32]
    mine = pl.ds(pl.multiple_of(where_ref[3] * 32, 32), 32)
    blocks[mine, :] = blocks[mine, :] + cross_ref[...] * factor
    out_ref[...] = blocks[...].astype(jnp.bfloat16)


def attend(where, q, other, summed, stat, cross):
    return pl.pallas_call(
        attend_kernel,
        out_shape=jax.ShapeDtypeStruct((QUERIES, HEAD_DIM), jnp.bfloat16),
        in_specs=[pl.BlockSpec(memory_space=pltpu.SMEM)] + [vmem()] * 5,
        out_specs=vmem(),
        scratch_shapes=[pltpu.VMEM((QUERIES, HEAD_DIM), jnp.float32)],
        compiler_params=params(),
        name="attend",
    )(where, q, other, summed, stat, cross)


def finish_kernel(parts_ref, latent_ref, guided_ref, next_ref):
    parts = parts_ref[...].astype(jnp.float32).reshape(64, 8, HEAD_DIM)
    summed = jnp.sum(parts, axis=0)
    columns = jnp.concatenate([summed] + [pltpu.roll(summed, HEAD_DIM - 32 * g, 1) for g in range(1, 4)], axis=0)
    guided = columns.T[0:32]
    guided_ref[...] = guided
    next_ref[...] = latent_ref[...] + STEP * guided


def finish(parts, latent):
    shape = jax.ShapeDtypeStruct(latent.shape, jnp.float32)
    return pl.pallas_call(
        finish_kernel,
        out_shape=(shape, shape),
        in_specs=[vmem()] * 2,
        out_specs=(vmem(), vmem()),
        compiler_params=params(),
        name="finish",
    )(parts, latent)


def back_groups():
    index = np.arange(512).reshape(2, SPREAD, 4, 2, 2)
    return [
        [int(index[f, z, x, c, h]) for z in BACK_PLANES for f in range(2) for h in range(2)]
        for x in range(4)
        for c in range(2)
    ]


def heads_first(block):
    return jnp.transpose(block, (1, 0, 2))


def shards(queries, self_keys, self_values, cross_queries, text_keys, text_values, out_weight, latent):
    w = jnp.transpose(out_weight, (0, 2, 1))
    packed = pack(heads_first(queries[0]), heads_first(self_keys[0]), heads_first(self_values[0]), w)
    recv = lax.all_to_all(packed, "z", 0, 0, tiled=True, axis_index_groups=[OUT_PLANES])
    crossed, zero = cross(heads_first(cross_queries[0]), heads_first(text_keys[0]), heads_first(text_values[0]), w)
    kv = jnp.broadcast_to(recv[None, :, 0:KV_ROWS, :], (4, SPREAD, KV_ROWS, HEAD_DIM))
    kv = jnp.where(zero[0] == 0, kv, jnp.zeros((), recv.dtype))
    own = lax.all_to_all(kv, "x", 0, 0, tiled=True).reshape(64, KV_ROWS, HEAD_DIM)
    left = lax.ppermute(recv[:, 0:24, :], "z", [(PLANES[3 * i + 1], PLANES[3 * i]) for i in range(5)])
    right = lax.ppermute(recv[:, 24:48, :], "z", [(PLANES[3 * i + 1], PLANES[3 * i + 2]) for i in range(5)])
    slot = lax.rem(lax.axis_index("z") + (SPREAD - FIRST_PLANE), SPREAD)
    moved = jnp.where(lax.rem(slot, 3) == 0, left, right)
    q = jnp.concatenate([recv[:, KV_ROWS:BLOCK, :], moved], axis=1)
    ready = moved[0:1, 0:1, :] == moved[0:1, 0:1, :]
    tile = jnp.where(ready, own[0:1, 0:16, :], jnp.zeros((), own.dtype))
    own = lax.dynamic_update_slice(own, tile, (0, 0, 0))
    other = lax.ppermute(own, "c", [(0, 1), (1, 0)])
    back_slot = lax.rem(lax.axis_index("z") + (SPREAD - BACK_PLANE), SPREAD)
    where = jnp.stack([slot, lax.axis_index("cfg"), lax.rem(slot, 3), back_slot]).astype(jnp.int32)
    summed, stat = first_half(q, own)
    back = attend(where, q, other, summed, stat, crossed)
    parts = lax.all_to_all(back, AXES, 0, 0, tiled=True, axis_index_groups=back_groups())
    return finish(parts, latent)


def solution(mesh):
    split = Mesh(mesh.devices.reshape(2, SPREAD, 4, 2, 2), ("cfg", "z", "x", "c", "head"))
    seq = ("z", "x", "c")
    tokens = P("cfg", seq, "head", None)
    text = P("cfg", None, "head", None)
    placed = (tokens, tokens, tokens, tokens, text, text, P("head", None, None), P(seq, "cfg"))
    return jax.shard_map(
        shards,
        mesh=split,
        in_specs=placed,
        out_specs=(P(seq, "cfg"), P(seq, "cfg")),
        check_vma=False,
    )
```

```python
import math

import jax
import jax.numpy as jnp
import numpy as np
from jax import lax
from jax.experimental import pallas as pl
from jax.experimental.pallas import tpu as pltpu
from jax.sharding import Mesh, PartitionSpec as P

HEAD_DIM = 128
HEADS_HERE = 10
ROWS = 32
SPREAD = 16
BLOCK = 56
KV_ROWS = 48
FIRST_PLANE = 11
BACK_PLANE = 9
PLANES = [(FIRST_PLANE + i) % SPREAD for i in range(SPREAD)]
BACK_PLANES = [(BACK_PLANE + i) % SPREAD for i in range(SPREAD)]
OUT_PLANES = [10, 9, 11, 8, 12, 7, 13, 6, 14, 5, 15, 4, 0, 3, 1, 2]
AXES = ("cfg", "z", "x", "c", "head")
GUIDANCE = 5.0
STEP = 0.1
EXP2_SCALE = math.log2(math.e) / math.sqrt(HEAD_DIM)
VMEM_LIMIT = 36 * 1024 * 1024


def vmem():
    return pl.BlockSpec(memory_space=pltpu.VMEM)


def params():
    return pltpu.CompilerParams(vmem_limit_bytes=VMEM_LIMIT)


def key_slot(head):
    return OUT_PLANES.index(PLANES[3 * (head // 2) + 2 * (head % 2)])


def query_slot(pair):
    return OUT_PLANES.index(PLANES[3 * pair + 1])


def pack_kernel(q_ref, k_ref, v_ref, w_ref, out_ref, blocks, q_scratch, k_scratch, v_scratch, w_scratch, sems):
    loads = [
        pltpu.make_async_copy(v_ref, v_scratch, sems.at[0]),
        pltpu.make_async_copy(w_ref, w_scratch, sems.at[1]),
        pltpu.make_async_copy(q_ref, q_scratch, sems.at[2]),
        pltpu.make_async_copy(k_ref, k_scratch, sems.at[3]),
    ]
    for load in loads:
        load.start()
    for pair in range(HEADS_HERE // 2):
        blocks[query_slot(pair), 48:BLOCK, :] = jnp.zeros((BLOCK - 48, HEAD_DIM), jnp.bfloat16)
    blocks[OUT_PLANES.index(PLANES[SPREAD - 1])] = jnp.zeros((BLOCK, HEAD_DIM), jnp.bfloat16)
    for load in loads:
        load.wait()
    for h in range(HEADS_HERE):
        blocks[key_slot(h), 0:32, :] = k_scratch[h]
        blocks[key_slot(h), KV_ROWS:BLOCK, :] = q_scratch[h, 0:8]
        blocks[query_slot(h // 2), 24 * (h % 2):24 * (h % 2) + 24, :] = q_scratch[h, 8:32]
        projected = lax.dot_general(
            v_scratch[h], w_scratch[h], (((1,), (1,)), ((), ())), preferred_element_type=jnp.float32
        )
        packed = jnp.concatenate([projected[0:16], projected[16:32]], axis=1)
        blocks[key_slot(h), 32:KV_ROWS, :] = packed.astype(jnp.bfloat16)
    store = pltpu.make_async_copy(blocks, out_ref, sems.at[4])
    store.start()
    store.wait()


def pack(q, k, v, w):
    anywhere = pl.BlockSpec(memory_space=pl.ANY)
    return pl.pallas_call(
        pack_kernel,
        out_shape=jax.ShapeDtypeStruct((SPREAD, BLOCK, HEAD_DIM), jnp.bfloat16),
        in_specs=[anywhere] * 4,
        out_specs=anywhere,
        scratch_shapes=[
            pltpu.VMEM((SPREAD, BLOCK, HEAD_DIM), jnp.bfloat16),
            pltpu.VMEM((HEADS_HERE, ROWS, HEAD_DIM), jnp.bfloat16),
            pltpu.VMEM((HEADS_HERE, ROWS, HEAD_DIM), jnp.bfloat16),
            pltpu.VMEM((HEADS_HERE, ROWS, HEAD_DIM), jnp.bfloat16),
            pltpu.VMEM((HEADS_HERE, 64, HEAD_DIM), jnp.bfloat16),
            pltpu.SemaphoreType.DMA((5,)),
        ],
        compiler_params=pltpu.CompilerParams(vmem_limit_bytes=60 * 1024 * 1024),
        name="pack",
    )(q, k, v, w)


def cross_kernel(q_ref, k_ref, v_ref, w_ref, sum_ref, zero_ref):
    total = jnp.zeros((ROWS, 64), jnp.float32)
    for h in range(HEADS_HERE):
        s = scores(q_ref[h], k_ref[h])
        top = jnp.max(s, axis=1, keepdims=True) * EXP2_SCALE
        p = jnp.exp2(s * EXP2_SCALE - top)
        o = jnp.dot(p.astype(jnp.bfloat16), v_ref[h], preferred_element_type=jnp.float32)
        o = o / jnp.sum(p, axis=1, keepdims=True)
        total = total + scores(o.astype(jnp.bfloat16), w_ref[h])
    columns = jnp.concatenate([total, jnp.zeros((ROWS, 64), jnp.float32)], axis=1).T
    columns = jnp.concatenate([columns, jnp.zeros((HEAD_DIM, HEAD_DIM - ROWS), jnp.float32)], axis=1)
    lane_group = lax.broadcasted_iota(jnp.int32, (8, HEAD_DIM), 1) // 32
    for half in range(2):
        block = columns[32 * half:32 * half + 8]
        for g in range(1, 4):
            piece = pltpu.roll(columns[32 * half + 8 * g:32 * half + 8 * g + 8], 32 * g, 1)
            block = jnp.where(lane_group == g, piece, block)
        sum_ref[16 * half:16 * half + 8, :] = block
        sum_ref[16 * half + 8:16 * half + 16, :] = block
    zero_ref[0] = 0


def cross(q, k, v, w):
    return pl.pallas_call(
        cross_kernel,
        out_shape=(
            jax.ShapeDtypeStruct((ROWS, HEAD_DIM), jnp.float32),
            jax.ShapeDtypeStruct((1,), jnp.int32),
        ),
        in_specs=[vmem()] * 4,
        out_specs=(vmem(), pl.BlockSpec(memory_space=pltpu.SMEM)),
        compiler_params=params(),
        cost_estimate=pl.CostEstimate(flops=90_000_000, bytes_accessed=3_200_000, transcendentals=170_000),
        name="cross",
    )(q, k, v, w)


def scores(q, keys):
    return lax.dot_general(q, keys, (((1,), (1,)), ((), ())), preferred_element_type=jnp.float32)


def load_keys(ref):
    even, odd = ref[:, 0:16, :], ref[:, 16:32, :]
    return [part.reshape(1024, HEAD_DIM) for part in (even, odd)], ref[:, 32:48, :].reshape(1024, HEAD_DIM)


def half_attention(q, keys, value, found_top=None):
    found = [scores(part, q) for part in keys]
    top = jnp.max(jnp.maximum(found[0], found[1]), axis=0, keepdims=True) * EXP2_SCALE
    if found_top is not None:
        top = jnp.maximum(top, found_top)
    weights = [jnp.exp2(s * EXP2_SCALE - top) for s in found]
    weight_sum = jnp.sum(weights[0] + weights[1], axis=0, keepdims=True)
    even, odd = [
        lax.dot_general(
            value, p.astype(jnp.bfloat16), (((0,), (0,)), ((), ())), preferred_element_type=jnp.float32
        )
        for p in weights
    ]
    return even[0:64] + odd[64:128], weight_sum, top


QUERIES = SPREAD * ROWS


def first_kernel(q_ref, own_ref, sum_ref, stat_ref):
    keys, value = load_keys(own_ref)
    summed, weight_sum, top = half_attention(q_ref[...].reshape(QUERIES, HEAD_DIM), keys, value)
    sum_ref[...] = summed
    stat_ref[0:8, :] = jnp.broadcast_to(weight_sum, (8, QUERIES))
    stat_ref[8:16, :] = jnp.broadcast_to(top, (8, QUERIES))


def first_half(q, own):
    return pl.pallas_call(
        first_kernel,
        out_shape=(
            jax.ShapeDtypeStruct((64, QUERIES), jnp.float32),
            jax.ShapeDtypeStruct((16, QUERIES), jnp.float32),
        ),
        in_specs=[vmem()] * 2,
        out_specs=(vmem(), vmem()),
        compiler_params=params(),
        cost_estimate=pl.CostEstimate(flops=540_000_000, bytes_accessed=1_600_000, transcendentals=1_000_000),
        name="first_half",
    )(q, own)


def attend_kernel(where_ref, q_ref, other_ref, sum_ref, stat_ref, cross_ref, out_ref, blocks):
    slot = where_ref[0]
    branch = where_ref[1]
    active = (slot < SPREAD - 1) & (where_ref[2] != 1)
    keys, value = load_keys(other_ref)
    first_sum, first_top = stat_ref[0:1, :], stat_ref[8:9, :]
    summed, weight_sum, top = half_attention(q_ref[...].reshape(QUERIES, HEAD_DIM), keys, value, first_top)
    scale = jnp.exp2(first_top - top)
    factor = jnp.where(branch == 0, GUIDANCE, 1.0 - GUIDANCE)
    total = (summed + sum_ref[...] * scale) * (factor / (weight_sum + first_sum * scale))
    total = jnp.where(active, total, 0.0)
    lane_group = lax.broadcasted_iota(jnp.int32, (32, HEAD_DIM), 1) // 32
    halves = []
    for half in range(2):
        groups = []
        for g in range(4):
            rows = total[32 * half + 8 * g:32 * half + 8 * g + 8]
            groups.append(jnp.concatenate([rows[:, 128 * t:128 * t + 128] for t in range(4)], axis=0))
        places = []
        for i in range(4):
            block = groups[i]
            for g in range(4):
                if g != i:
                    block = jnp.where(lane_group == g, pltpu.roll(groups[g], 32 * ((g - i) % 4), 1), block)
            places.append(block.reshape(4, 1, 1, 8, HEAD_DIM))
        halves.append(jnp.concatenate(places, axis=1))
    packed = jnp.concatenate([halves[0], halves[0], halves[1], halves[1]], axis=2).reshape(QUERIES, HEAD_DIM)
    for at, plane in enumerate(BACK_PLANES):
        held = 32 * OUT_PLANES.index(plane)
        blocks[32 * at:32 * at + 32, :] = packed[held:held + 32]
    mine = pl.ds(pl.multiple_of(where_ref[3] * 32, 32), 32)
    blocks[mine, :] = blocks[mine, :] + cross_ref[...] * factor
    out_ref[...] = blocks[...].astype(jnp.bfloat16)


def attend(where, q, other, summed, stat, cross):
    return pl.pallas_call(
        attend_kernel,
        out_shape=jax.ShapeDtypeStruct((QUERIES, HEAD_DIM), jnp.bfloat16),
        in_specs=[pl.BlockSpec(memory_space=pltpu.SMEM)] + [vmem()] * 5,
        out_specs=vmem(),
        scratch_shapes=[pltpu.VMEM((QUERIES, HEAD_DIM), jnp.float32)],
        compiler_params=params(),
        name="attend",
    )(where, q, other, summed, stat, cross)


def finish_kernel(parts_ref, latent_ref, guided_ref, next_ref):
    parts = parts_ref[...].astype(jnp.float32).reshape(64, 8, HEAD_DIM)
    summed = jnp.sum(parts, axis=0)
    columns = jnp.concatenate([summed] + [pltpu.roll(summed, HEAD_DIM - 32 * g, 1) for g in range(1, 4)], axis=0)
    guided = columns.T[0:32]
    guided_ref[...] = guided
    next_ref[...] = latent_ref[...] + STEP * guided


def finish(parts, latent):
    shape = jax.ShapeDtypeStruct(latent.shape, jnp.float32)
    return pl.pallas_call(
        finish_kernel,
        out_shape=(shape, shape),
        in_specs=[vmem()] * 2,
        out_specs=(vmem(), vmem()),
        compiler_params=params(),
        name="finish",
    )(parts, latent)


def back_groups():
    index = np.arange(512).reshape(2, SPREAD, 4, 2, 2)
    return [
        [int(index[f, z, x, c, h]) for z in BACK_PLANES for f in range(2) for h in range(2)]
        for x in range(4)
        for c in range(2)
    ]


def heads_first(block):
    return jnp.transpose(block, (1, 0, 2))


def shards(queries, self_keys, self_values, cross_queries, text_keys, text_values, out_weight, latent):
    w = jnp.transpose(out_weight, (0, 2, 1))
    packed = pack(heads_first(queries[0]), heads_first(self_keys[0]), heads_first(self_values[0]), w)
    recv = lax.all_to_all(packed, "z", 0, 0, tiled=True, axis_index_groups=[OUT_PLANES])
    crossed, zero = cross(heads_first(cross_queries[0]), heads_first(text_keys[0]), heads_first(text_values[0]), w)
    kv = jnp.broadcast_to(recv[None, :, 0:KV_ROWS, :], (4, SPREAD, KV_ROWS, HEAD_DIM))
    kv = jnp.where(zero[0] == 0, kv, jnp.zeros((), recv.dtype))
    own = lax.all_to_all(kv, "x", 0, 0, tiled=True).reshape(64, KV_ROWS, HEAD_DIM)
    left = lax.ppermute(recv[:, 0:24, :], "z", [(PLANES[3 * i + 1], PLANES[3 * i]) for i in range(5)])
    right = lax.ppermute(recv[:, 24:48, :], "z", [(PLANES[3 * i + 1], PLANES[3 * i + 2]) for i in range(5)])
    slot = lax.rem(lax.axis_index("z") + (SPREAD - FIRST_PLANE), SPREAD)
    moved = jnp.where(lax.rem(slot, 3) == 0, left, right)
    q = jnp.concatenate([recv[:, KV_ROWS:BLOCK, :], moved], axis=1)
    ready = moved[0:1, 0:1, :] == moved[0:1, 0:1, :]
    tile = jnp.where(ready, own[0:1, 0:16, :], jnp.zeros((), own.dtype))
    own = lax.dynamic_update_slice(own, tile, (0, 0, 0))
    other = lax.ppermute(own, "c", [(0, 1), (1, 0)])
    back_slot = lax.rem(lax.axis_index("z") + (SPREAD - BACK_PLANE), SPREAD)
    where = jnp.stack([slot, lax.axis_index("cfg"), lax.rem(slot, 3), back_slot]).astype(jnp.int32)
    summed, stat = first_half(q, own)
    back = attend(where, q, other, summed, stat, crossed)
    parts = lax.all_to_all(back, AXES, 0, 0, tiled=True, axis_index_groups=back_groups())
    return finish(parts, latent)


def solution(mesh):
    split = Mesh(mesh.devices.reshape(2, SPREAD, 4, 2, 2), ("cfg", "z", "x", "c", "head"))
    seq = ("z", "x", "c")
    tokens = P("cfg", seq, "head", None)
    text = P("cfg", None, "head", None)
    placed = (tokens, tokens, tokens, tokens, text, text, P("head", None, None), P(seq, "cfg"))
    return jax.shard_map(
        shards,
        mesh=split,
        in_specs=placed,
        out_specs=(P(seq, "cfg"), P(seq, "cfg")),
        check_vma=False,
    )
```
